32 devices in a mesh: groups: 2 (over x), dp: 8 (over z, y), tensor: 2 (over core).
Axes of the slice: x: 2, y: 2, z: 4, core: 2. Of those that a mesh axis runs over, the one named last changes fastest.
Arguments:
- acts: bfloat16 [4, 2048, 4096], P('groups', 'dp'), parts along dimension 0, may hold values from -6 to 6
- grad_query: bfloat16 [4, 2048, 8192], P('groups', 'dp', 'tensor'), parts along dimension 0, may hold values from -6 to 6
- keyvalue_gradient: bfloat16 [4, 2048, 2, 512], P('groups', 'dp', None, 'tensor'), parts along dimension 0, may hold values from -6 to 6
- attn_out: bfloat16 [4, 2048, 8192], P('groups', 'dp', 'tensor'), parts along dimension 0, may hold values from -6 to 6
- grad_out: bfloat16 [4, 2048, 4096], P('groups', 'dp'), parts along dimension 0, may hold values from -6 to 6
- seq_lengths: int32 [8, 16], P('dp', 'groups'), parts along dimension 1, may hold values from 1 to 64, 256 in all within a row
- group_ids: int32 [8, 16], P('dp', 'groups'), parts along dimension 1, may hold values from 0 to 1
- rewards: float32 [8, 16], P('dp', 'groups'), parts along dimension 1, may hold values from -8 to 8
- wide_params: float32 [4, 4096, 256], P('groups', ('dp', 'tensor')), parts along dimension 0, may hold values from -0.3 to 0.3
- wide_moments: float32 [2, 4, 4096, 256], P(None, 'groups', ('dp', 'tensor')), parts along dimension 1, may hold values from -4 to 4, as said below
- head_params: float32 [4, 64, 128, 128], P('groups', 'tensor', 'dp'), parts along dimension 0, may hold values from -0.3 to 0.3
- head_moments: float32 [2, 4, 64, 128, 128], P(None, 'groups', 'tensor', 'dp'), parts along dimension 1, may hold values from -4 to 4, as said below
- key_value_adapters: float32 [4, 4, 128, 128], P('groups', 'tensor', 'dp'), parts along dimension 0, may hold values from -0.3 to 0.3
- kv_moments: float32 [2, 4, 4, 128, 128], P(None, 'groups', 'tensor', 'dp'), parts along dimension 1, may hold values from -4 to 4, as said below
- base_query: bfloat16 [2, 64, 128, 4096], P(None, 'tensor', None, 'dp'), may hold values from -0.1796875 to 0.1796875
- frozen_key_rows: bfloat16 [2, 4, 128, 4096], P(None, 'tensor', None, 'dp'), may hold values from -0.1796875 to 0.1796875
- rotary_rows: int32 [128], replicated, may hold values from 0 to 127, each once
- rollout_group_order: int32 [4], replicated, may hold values from 0 to 3, each once
Outputs:
- new_wide: float32 [4, 4096, 256], P('groups', ('dp', 'tensor')), parts along dimension 0
- new_wide_moments: float32 [2, 4, 4096, 256], P(None, 'groups', ('dp', 'tensor')), parts along dimension 1
- new_head: float32 [4, 64, 128, 128], P('groups', 'tensor', 'dp'), parts along dimension 0
- new_head_moments: float32 [2, 4, 64, 128, 128], P(None, 'groups', 'tensor', 'dp'), parts along dimension 1
- new_kv: float32 [4, 4, 128, 128], P('groups', 'tensor', 'dp'), parts along dimension 0
- new_kv_moments: float32 [2, 4, 4, 128, 128], P(None, 'groups', 'tensor', 'dp'), parts along dimension 1
- merged_query: bfloat16 [4, 64, 128, 4096], P('groups', 'tensor', None, 'dp'), parts along dimension 0
- merged_key: bfloat16 [4, 4, 128, 4096], P('groups', 'tensor', None, 'dp'), parts along dimension 0
The draws below stay inside these ranges and needn't reach their ends.
There are 2 independent parts, one for each index of `groups`. The reference program is written for one: setup_inputs(seed, part) draws one part's arguments, and reference() takes and returns one part's arrays. A program takes and returns all parts, laid end to end along the dimension named above; an argument that names none is the same for every part. Nothing has to cross between parts.
Inputs may be any that keep to these rules, and one draw needn't show every extreme that they name: `seq_lengths`: each row sums to 256, and one sequence of every row has exactly 64 tokens. `rotary_rows`: a permutation. `rollout_group_order`: a permutation. `wide_moments`: entry 0 holds first moments, entry 1 positive second moments. `head_moments`: entry 0 holds first moments, entry 1 positive second moments. `kv_moments`: entry 0 holds first moments, entry 1 positive second moments.
All inputs are finite; a program needn't handle non-finite values.
Results may differ from the reference program's by a relative error of at most 0.0059.
Values may be sent and summed in bfloat16 or wider, within the bound.
A program may use at most 192 MiB of HBM per device.

```python
import math
import jax
import jax.numpy as jnp
import numpy as np
from jax import lax

MODEL_DIM = 4096
QUERY_HEADS = 64
KEY_HEADS = 4
HEAD_SIZE = 128
ADAPTER_RANK = 64
LAYER_COUNT = 2
TOK_DEV = 256
SEQ_DEV = 8
GROUPS = 2
BLOCKS = 8
TOKEN_TOTAL = 2048


def moment_couple(key, shape):
    first_moment = jnp.clip(jax.random.normal(jax.random.fold_in(key, 11), shape, jnp.float32), -4.0, 4.0)
    second_moment = jnp.exp(jax.random.uniform(jax.random.fold_in(key, 12), shape, jnp.float32, math.log(0.5), math.log(4.0)))
    return jnp.stack([first_moment, second_moment])


def draw_wide_moments(key, part):
    key = jax.random.fold_in(key, 1)
    return moment_couple(key, (LAYER_COUNT, MODEL_DIM, 4 * ADAPTER_RANK))


def draw_head_moments(key, part):
    key = jax.random.fold_in(key, 2)
    return moment_couple(key, (LAYER_COUNT, QUERY_HEADS, HEAD_SIZE, 2 * ADAPTER_RANK))


def draw_kv_moments(key, part):
    key = jax.random.fold_in(key, 3)
    return moment_couple(key, (LAYER_COUNT, KEY_HEADS, HEAD_SIZE, 2 * ADAPTER_RANK))


def with_ends(array, stream_key, low, high):
    dims = array.shape
    spot = [jax.random.randint(jax.random.fold_in(stream_key, axis), (), 0, dims[axis]) for axis in range(len(dims))]
    array = array.at[tuple(spot)].set(low)
    longest = dims.index(max(dims))
    spot[longest] = (spot[longest] + 1) % dims[longest]
    return array.at[tuple(spot)].set(high)


def block_levels(stream_key, extent, cuts, smallest, largest):
    def one(axis_at, shards_of):
        draws = jax.random.uniform(jax.random.fold_in(jax.random.fold_in(stream_key, 6), axis_at), (shards_of,), jnp.float32, smallest / len(cuts), largest / len(cuts))
        return jnp.repeat(jnp.exp(draws), extent[axis_at] // shards_of).reshape((-1,) + (1,) * (len(extent) - axis_at - 1))

    loudness = one(*cuts[0])
    for cut in cuts[1:]:
        loudness = loudness * one(*cut)
    return loudness


def profile(number_of, total, most, slope):
    portions = [(1 << 20) // math.isqrt(rank ** slope) + 1 for rank in range(2, number_of + 1)]
    rest, counts = total - most - (number_of - 1), [1] * (number_of - 1)
    while rest > 0:
        candidates = [i for i in range(number_of - 1) if counts[i] < most]
        whole, budget = sum([portions[i] for i in candidates]), rest
        for i in candidates:
            more = min(most - counts[i], max(1, budget * portions[i] // whole), rest)
            counts[i] = counts[i] + more
            rest = rest - more
    return np.array([most] + counts)


def uneven(rng, amount, total, limit, lean):
    if amount == 2:
        one = jax.random.randint(rng, (), max(1, total - limit), min(limit, total - 1) + 1)
        return jnp.stack([one, total - one])
    sizes = jnp.asarray(profile(amount, total, limit, lean), jnp.int32)
    pairs = (amount - 1) // 2
    source_of, taker = sizes[1:1 + 2 * pairs:2], sizes[2:2 + 2 * pairs:2]
    slack = jnp.minimum(source_of - 1, limit - taker)
    passed = jax.random.randint(jax.random.fold_in(rng, 1), (pairs,), 0, 1 << 20) % (slack + 1)
    sizes = sizes.at[1:1 + 2 * pairs:2].set(source_of - passed).at[2:2 + 2 * pairs:2].set(taker + passed)
    return sizes[jax.random.permutation(jax.random.fold_in(rng, 2), amount)]


def scatter_about(key, extent, deviation, reach, split=(), held_as=jnp.bfloat16):
    level = block_levels(key, extent, split, -0.22, 0.18) if split else 1.0
    values = jax.random.normal(key, extent, jnp.float32) * deviation * level
    return jnp.minimum(jnp.maximum(values, -reach), reach).astype(held_as)


def setup_inputs(seed: int = 0, part: int = 0) -> dict:
    key_of = jax.random.split(jax.random.key(seed), 19)
    part_splits = jax.random.split(jax.random.fold_in(key_of[18], part), 19)
    return {
        "acts": scatter_about(part_splits[0], (LAYER_COUNT, TOKEN_TOTAL, MODEL_DIM), 1.0, 6.0, ((1, 8),)),
        "grad_query": scatter_about(part_splits[1], (LAYER_COUNT, TOKEN_TOTAL, QUERY_HEADS * HEAD_SIZE), 1.0, 6.0, ((1, 8), (2, 2))),
        "keyvalue_gradient": scatter_about(part_splits[2], (LAYER_COUNT, TOKEN_TOTAL, 2, KEY_HEADS * HEAD_SIZE), 1.0, 6.0, ((1, 8), (3, 2))),
        "attn_out": scatter_about(part_splits[3], (LAYER_COUNT, TOKEN_TOTAL, QUERY_HEADS * HEAD_SIZE), 1.0, 6.0, ((1, 8), (2, 2))),
        "grad_out": scatter_about(part_splits[4], (LAYER_COUNT, TOKEN_TOTAL, MODEL_DIM), 1.0, 6.0, ((1, 8),)),
        "seq_lengths": jax.vmap(lambda own: uneven(own, SEQ_DEV, TOK_DEV, TOK_DEV // 4, 1))(jax.random.split(part_splits[5], BLOCKS)).reshape((BLOCKS, SEQ_DEV)).astype(jnp.int32),
        "group_ids": with_ends(jax.random.randint(part_splits[6], (BLOCKS, SEQ_DEV), 0, GROUPS), jax.random.fold_in(part_splits[6], 1), 0, GROUPS - 1).astype(jnp.int32),
        "rewards": scatter_about(part_splits[7], (BLOCKS, SEQ_DEV), 2.0, 8.0, ((0, 8),), jnp.float32),
        "wide_params": scatter_about(part_splits[8], (LAYER_COUNT, MODEL_DIM, 4 * ADAPTER_RANK), 0.05, 0.3, ((1, 16),), jnp.float32),
        "wide_moments": draw_wide_moments(jax.random.fold_in(jax.random.fold_in(key_of[18], part), 71), part),
        "head_params": scatter_about(part_splits[10], (LAYER_COUNT, QUERY_HEADS, HEAD_SIZE, 2 * ADAPTER_RANK), 0.05, 0.3, ((1, 2), (2, 8)), jnp.float32),
        "head_moments": draw_head_moments(jax.random.fold_in(jax.random.fold_in(key_of[18], part), 71), part),
        "key_value_adapters": scatter_about(part_splits[12], (LAYER_COUNT, KEY_HEADS, HEAD_SIZE, 2 * ADAPTER_RANK), 0.05, 0.3, ((1, 2), (2, 8)), jnp.float32),
        "kv_moments": draw_kv_moments(jax.random.fold_in(jax.random.fold_in(key_of[18], part), 71), part),
        "base_query": scatter_about(key_of[14], (LAYER_COUNT, QUERY_HEADS, HEAD_SIZE, MODEL_DIM), 0.03, 0.1796875, ((1, 2), (3, 8))),
        "frozen_key_rows": scatter_about(key_of[15], (LAYER_COUNT, KEY_HEADS, HEAD_SIZE, MODEL_DIM), 0.03, 0.1796875, ((1, 2), (3, 8))),
        "rotary_rows": jax.random.permutation(key_of[16], HEAD_SIZE).astype(jnp.int32),
        "rollout_group_order": jax.random.permutation(key_of[17], KEY_HEADS).astype(jnp.int32),
    }


adapter_scale = 2.0
beta_one = 0.9
beta_two = 0.99
learn_rate = 0.002
decay_rate = 0.01
adam_eps = 1e-08
bias_one = 1.0 - beta_one ** 20
bias_two = 1.0 - beta_two ** 20

def token_weights(seq_lengths, group_ids, rewards, count):
    seq_ends = jnp.cumsum(seq_lengths, axis=-1).astype(jnp.int32)
    starts = seq_ends - seq_lengths
    places = jnp.arange(count, dtype=jnp.int32)
    member = ((places[None, :, None] >= starts[:, None, :]) & (places[None, :, None] < seq_ends[:, None, :])).astype(jnp.float32)
    same_group = (group_ids[:, :, None] == group_ids[:, None, :]).astype(jnp.float32)
    group_mean = lax.optimization_barrier(jnp.sum(same_group * rewards[:, None, :], axis=-1)) / lax.optimization_barrier(jnp.sum(same_group, axis=-1))
    advantage = rewards - group_mean
    per_seq = advantage / seq_lengths.astype(jnp.float32)
    return lax.optimization_barrier(jnp.sum(member * per_seq[:, None, :], axis=-1)).reshape(-1)

def contracted_rows(left, right):
    return lax.dot_general(left, right, (((0,), (0,)), ((), ())), preferred_element_type=jnp.float32)

def layer_grads(input_rows, query_gradient, keyval_grad, attention_piece, output_gradient, work_wide, work_head, work_kv, weight_col):
    adapter_rank_size = work_wide.shape[1] // 4
    a_in = work_wide[:, :3 * adapter_rank_size]
    b_out = work_wide[:, 3 * adapter_rank_size:]
    flat_head = work_head.reshape(-1, 2 * adapter_rank_size)
    flat_kv = work_kv.reshape(-1, 2 * adapter_rank_size)
    key_gradient = keyval_grad[:, 0]
    value_gradient = keyval_grad[:, 1]
    hidden_weighted = (weight_col * jnp.dot(input_rows, a_in, preferred_element_type=jnp.float32)).astype(jnp.bfloat16)
    g_sum = jnp.concatenate([jnp.dot(query_gradient, flat_head[:, :adapter_rank_size], preferred_element_type=jnp.float32), jnp.dot(key_gradient, flat_kv[:, :adapter_rank_size], preferred_element_type=jnp.float32), jnp.dot(value_gradient, flat_kv[:, adapter_rank_size:], preferred_element_type=jnp.float32)], axis=1)
    gate_weighted = (weight_col * g_sum).astype(jnp.bfloat16)
    hidden_output = (weight_col * jnp.dot(attention_piece, flat_head[:, adapter_rank_size:], preferred_element_type=jnp.float32)).astype(jnp.bfloat16)
    gate_output = (weight_col * jnp.dot(output_gradient, b_out, preferred_element_type=jnp.float32)).astype(jnp.bfloat16)
    wide_gradient = adapter_scale * jnp.concatenate([contracted_rows(input_rows, gate_weighted), contracted_rows(output_gradient, hidden_output)], axis=1)
    head_gradient = adapter_scale * jnp.concatenate([contracted_rows(query_gradient, hidden_weighted[:, :adapter_rank_size]), contracted_rows(attention_piece, gate_output)], axis=1)
    key_value_gradient = adapter_scale * jnp.concatenate([contracted_rows(key_gradient, hidden_weighted[:, adapter_rank_size:2 * adapter_rank_size]), contracted_rows(value_gradient, hidden_weighted[:, 2 * adapter_rank_size:])], axis=1)
    return (wide_gradient, head_gradient.reshape(work_head.shape), key_value_gradient.reshape(work_kv.shape))

def adamw(parameter, moments, gradient):
    first_moment = beta_one * moments[0] + (1.0 - beta_one) * gradient
    second_moment = beta_two * moments[1] + (1.0 - beta_two) * gradient * gradient
    update = first_moment / bias_one / (jnp.sqrt(second_moment / bias_two) + adam_eps)
    return (parameter - learn_rate * (update + decay_rate * parameter), jnp.stack([first_moment, second_moment]))

def merged_rows(base_rows, rank_up, rank_down, row_order, head_index):
    selected_frozen = jnp.take(jnp.take(base_rows, head_index, axis=1), row_order, axis=2)
    picked_up = jnp.take(jnp.take(rank_up, head_index, axis=1), row_order, axis=2)
    low_rank_product = jnp.einsum('lhjr,ldr->lhjd', picked_up.astype(jnp.float32), rank_down.astype(jnp.float32))
    return (selected_frozen.astype(jnp.float32) + adapter_scale * low_rank_product).astype(jnp.bfloat16)

def reference(acts, grad_query, keyvalue_gradient, attn_out, grad_out, seq_lengths, group_ids, rewards, wide_params, wide_moments, head_params, head_moments, key_value_adapters, kv_moments, base_query, frozen_key_rows, rotary_rows, rollout_group_order):
    weight_col = token_weights(seq_lengths, group_ids, rewards, TOK_DEV)[:, None]
    work_wide = wide_params.astype(jnp.bfloat16)
    work_head = head_params.astype(jnp.bfloat16)
    work_kv = key_value_adapters.astype(jnp.bfloat16)
    wide_list = []
    head_list = []
    kv_list = []
    for layer_num in range(LAYER_COUNT):
        wide_gradient, head_gradient, key_value_gradient = layer_grads(acts[layer_num], grad_query[layer_num], keyvalue_gradient[layer_num], attn_out[layer_num], grad_out[layer_num], work_wide[layer_num], work_head[layer_num], work_kv[layer_num], weight_col)
        wide_list.append(wide_gradient)
        head_list.append(head_gradient)
        kv_list.append(key_value_gradient)
    new_wide, new_wide_moments = adamw(wide_params, wide_moments, jnp.stack(wide_list))
    new_head, new_head_moments = adamw(head_params, head_moments, jnp.stack(head_list))
    new_kv, new_kv_moments = adamw(key_value_adapters, kv_moments, jnp.stack(kv_list))
    rank_a = new_wide[..., :2 * ADAPTER_RANK].astype(jnp.bfloat16)
    rank_bq = new_head[..., :ADAPTER_RANK].astype(jnp.bfloat16)
    rank_bk = new_kv[..., :ADAPTER_RANK].astype(jnp.bfloat16)
    group_width = QUERY_HEADS // KEY_HEADS
    slots = jnp.arange(QUERY_HEADS, dtype=jnp.int32)
    query_heads = (jnp.take(rollout_group_order, slots // group_width) * group_width + slots % group_width).astype(jnp.int32)
    merged_query = merged_rows(base_query, rank_bq, rank_a[..., :ADAPTER_RANK], rotary_rows, query_heads)
    merged_key = merged_rows(frozen_key_rows, rank_bk, rank_a[..., ADAPTER_RANK:2 * ADAPTER_RANK], rotary_rows, rollout_group_order)
    return (new_wide, new_wide_moments, new_head, new_head_moments, new_kv, new_kv_moments, merged_query, merged_key)
```

```python
import functools

import jax
import jax.numpy as jnp
from jax import lax
from jax.experimental import pallas as pl
from jax.experimental.pallas import tpu as pltpu
from jax.sharding import PartitionSpec as P

adapter_scale = 2.0
beta_one = 0.9
beta_two = 0.99
learn_rate = 0.002
decay_rate = 0.01
adam_eps = 1e-08
bias_one = 1.0 - beta_one**20
bias_two = 1.0 - beta_two**20


def token_weights(seq_lengths, group_ids, rewards, count):
    seq_ends = jnp.cumsum(seq_lengths, axis=-1)
    starts = seq_ends - seq_lengths
    places = jnp.arange(count, dtype=jnp.int32)
    member = (
        (places[None, :, None] >= starts[:, None, :])
        & (places[None, :, None] < seq_ends[:, None, :])
    ).astype(jnp.float32)
    same_group = (group_ids[:, :, None] == group_ids[:, None, :]).astype(jnp.float32)
    group_mean = jnp.sum(same_group * rewards[:, None, :], axis=-1) / jnp.sum(same_group, axis=-1)
    advantage = rewards - group_mean
    per_seq = advantage / seq_lengths.astype(jnp.float32)
    return jnp.sum(member * per_seq[:, None, :], axis=-1).reshape(-1)


def contracted_rows(left, right):
    return lax.dot_general(
        left, right, (((0,), (0,)), ((), ())), preferred_element_type=jnp.float32
    )


def adamw(parameter, moments, gradient):
    first_moment = beta_one * moments[0] + (1.0 - beta_one) * gradient
    second_moment = beta_two * moments[1] + (1.0 - beta_two) * gradient * gradient
    update = first_moment / bias_one / (jnp.sqrt(second_moment / bias_two) + adam_eps)
    return (
        parameter - learn_rate * (update + decay_rate * parameter),
        jnp.stack([first_moment, second_moment]),
    )


MESH = pl.DeviceIdType.MESH
ROW_STEP = 32


def remote(src, dst, send_sem, recv_sem, device):
    return pltpu.make_async_remote_copy(
        src_ref=src,
        dst_ref=dst,
        send_sem=send_sem,
        recv_sem=recv_sem,
        device_id=device,
        device_id_type=MESH,
    )


def place(count):
    me = lax.axis_index("dp")
    return me, me // 2, me % 2, count // 2


def greet(z, m, partners):
    me = lax.axis_index("dp")
    barrier = pltpu.get_barrier_semaphore()
    for device in partners:
        pl.semaphore_signal(barrier, inc=1, device_id=device, device_id_type=MESH)

    @pl.when(z > 0)
    def _():
        pl.semaphore_signal(barrier, inc=1, device_id={"dp": me - 2}, device_id_type=MESH)

    @pl.when(z < m - 1)
    def _():
        pl.semaphore_signal(barrier, inc=1, device_id={"dp": me + 2}, device_id_type=MESH)

    ends = jnp.where(z > 0, 1, 0) + jnp.where(z < m - 1, 1, 0)
    pl.semaphore_wait(barrier, len(partners) + ends)


def gather_kernel(count, pieces, share, swaps, *refs):
    refs = list(refs)
    take = lambda k: [refs.pop(0) for _ in range(k)]
    ins, swap_ins = take(pieces), take(swaps)
    outs, others, swap_outs = take(pieces), take(pieces if share else 0), take(swaps)
    send_right, send_left, send_row, recv, local_sem = take(5)
    send_core, recv_core = take(2) if share else (None, None)
    send_swap, recv_swap = take(2) if swaps else (None, None)
    me, z, y, m = place(count)
    row_mate = {"dp": me + 1 - 2 * y}
    core_mate = {"tensor": 1 - lax.axis_index("tensor")}
    has_left, has_right = z > 0, z < m - 1
    greet(z, m, [row_mate] + ([core_mate] if share or swaps else []))

    def right(p, src, k):
        slot = (z - k) * 2 + y
        return remote(src(slot), outs[p].at[slot], send_right.at[p, k], recv.at[p, slot], {"dp": me + 2})

    def left(p, src, k):
        slot = (z + k) * 2 + y
        return remote(src(slot), outs[p].at[slot], send_left.at[p, k], recv.at[p, slot], {"dp": me - 2})

    def across(p, src, zz):
        slot = zz * 2 + y
        return remote(src(slot), outs[p].at[slot], send_row.at[p, zz], recv.at[p, slot], row_mate)

    def to_core(p, src, slot):
        return remote(src(slot), others[p].at[slot], send_core.at[p, slot], recv_core.at[p, slot], core_mate)

    def arrive(p, slot):
        remote(outs[p].at[slot], outs[p].at[slot], send_row.at[p, 0], recv.at[p, slot], row_mate).wait_recv()

    own = [lambda slot, r=r: r for r in ins]
    held = [lambda slot, r=r: r.at[slot] for r in outs]

    for s in range(swaps):
        remote(swap_ins[s], swap_outs[s], send_swap.at[s], recv_swap.at[s], core_mate).start()
    for p in range(pieces):

        @pl.when(has_right)
        def _():
            right(p, own[p], 0).start()

        @pl.when(has_left)
        def _():
            left(p, own[p], 0).start()

        across(p, own[p], z).start()
        if share:
            to_core(p, own[p], me).start()
        pltpu.make_async_copy(ins[p], outs[p].at[me], local_sem.at[p]).start()

    for k in range(1, m):
        for p in range(pieces):

            @pl.when(z - k >= 0)
            def _():
                slot = (z - k) * 2 + y
                arrive(p, slot)

                @pl.when(has_right)
                def _():
                    right(p, held[p], k).start()

                across(p, held[p], z - k).start()
                if share:
                    to_core(p, held[p], slot).start()

            @pl.when(z + k < m)
            def _():
                slot = (z + k) * 2 + y
                arrive(p, slot)

                @pl.when(has_left)
                def _():
                    left(p, held[p], k).start()

                across(p, held[p], z + k).start()
                if share:
                    to_core(p, held[p], slot).start()

    far = 1 - y
    for zz in range(m):
        for p in range(pieces):
            slot = zz * 2 + far
            arrive(p, slot)
            if share:
                to_core(p, held[p], slot).start()
    for p in range(pieces):
        pltpu.make_async_copy(ins[p], outs[p].at[me], local_sem.at[p]).wait()
        for zz in range(m):
            across(p, held[p], zz).wait_send()
        for k in range(m):

            @pl.when(has_right & (z - k >= 0))
            def _():
                right(p, held[p], k).wait_send()

            @pl.when(has_left & (z + k < m))
            def _():
                left(p, held[p], k).wait_send()

        if share:
            for slot in range(count):
                to_core(p, held[p], slot).wait()
    for s in range(swaps):
        remote(swap_ins[s], swap_outs[s], send_swap.at[s], recv_swap.at[s], core_mate).wait()


def gather_dp(arrays, swapped, count, share, collective_id):
    pieces, swaps, m = len(arrays), len(swapped), count // 2
    stacked = [jax.ShapeDtypeStruct((count,) + a.shape, a.dtype) for a in arrays]
    dma = pltpu.SemaphoreType.DMA
    scratch = [dma((pieces, m)), dma((pieces, m)), dma((pieces, m)), dma((pieces, count)), dma((pieces,))]
    if share:
        scratch += [dma((pieces, count)), dma((pieces, count))]
    if swaps:
        scratch += [dma((swaps,)), dma((swaps,))]
    shapes = stacked + (stacked if share else []) + [
        jax.ShapeDtypeStruct(a.shape, a.dtype) for a in swapped
    ]
    anywhere = pl.BlockSpec(memory_space=pl.ANY)
    return pl.pallas_call(
        functools.partial(gather_kernel, count, pieces, share, swaps),
        out_shape=shapes,
        in_specs=[anywhere] * (pieces + swaps),
        out_specs=[anywhere] * len(shapes),
        scratch_shapes=scratch,
        compiler_params=pltpu.CompilerParams(collective_id=collective_id, has_side_effects=True),
        name="gather_pieces",
    )(*arrays, *swapped)


def add_rows(dst, terms):
    def step(i, carry):
        rows = pl.ds(pl.multiple_of(i * ROW_STEP, ROW_STEP), ROW_STEP)
        total = terms[0][rows, :].astype(jnp.float32)
        for term in terms[1:]:
            total = total + term[rows, :].astype(jnp.float32)
        dst[rows, :] = total.astype(dst.dtype)
        return carry

    lax.fori_loop(0, dst.shape[0] // ROW_STEP, step, 0)


def scatter_kernel(count, pieces, *refs):
    refs = list(refs)
    take = lambda k: [refs.pop(0) for _ in range(k)]
    ins, outs = take(pieces), take(pieces)
    from_row, from_left, from_right, leaving = take(pieces), take(pieces), take(pieces), take(pieces)
    row_send, row_recv, line_send, left_recv, right_recv = take(5)
    me, z, y, m = place(count)
    row_mate = {"dp": me + 1 - 2 * y}
    has_left, has_right = z > 0, z < m - 1
    greet(z, m, [row_mate])

    def across(p, zz):
        return remote(
            ins[p].at[zz * 2 + 1 - y], from_row[p].at[zz], row_send.at[p, zz], row_recv.at[p, zz], row_mate
        )

    def right(p, zz):
        return remote(
            leaving[p].at[zz], from_left[p].at[zz], line_send.at[p, zz], left_recv.at[p, zz], {"dp": me + 2}
        )

    def left(p, zz):
        return remote(
            leaving[p].at[zz], from_right[p].at[zz], line_send.at[p, zz], right_recv.at[p, zz], {"dp": me - 2}
        )

    for k in range(m - 1, 0, -1):
        for p in range(pieces):

            @pl.when(z + k < m)
            def _():
                across(p, z + k).start()

            @pl.when(z - k >= 0)
            def _():
                across(p, z - k).start()

    for p in range(pieces):
        across(p, z).start()

    for k in range(m - 1, 0, -1):
        for p in range(pieces):

            @pl.when(z + k < m)
            def _():
                zz = z + k
                across(p, zz).wait_recv()
                near = [ins[p].at[zz * 2 + y], from_row[p].at[zz]]

                @pl.when(has_left)
                def _():
                    right(p, zz).wait_recv()
                    add_rows(leaving[p].at[zz], near + [from_left[p].at[zz]])

                @pl.when(jnp.logical_not(has_left))
                def _():
                    add_rows(leaving[p].at[zz], near)

                right(p, zz).start()

            @pl.when(z - k >= 0)
            def _():
                zz = z - k
                across(p, zz).wait_recv()
                near = [ins[p].at[zz * 2 + y], from_row[p].at[zz]]

                @pl.when(has_right)
                def _():
                    left(p, zz).wait_recv()
                    add_rows(leaving[p].at[zz], near + [from_right[p].at[zz]])

                @pl.when(jnp.logical_not(has_right))
                def _():
                    add_rows(leaving[p].at[zz], near)

                left(p, zz).start()

    for p in range(pieces):
        across(p, z).wait_recv()
        add_rows(outs[p], [ins[p].at[me], from_row[p].at[z]])

        @pl.when(has_left)
        def _():
            right(p, z).wait_recv()
            add_rows(outs[p], [outs[p], from_left[p].at[z]])

        @pl.when(has_right)
        def _():
            left(p, z).wait_recv()
            add_rows(outs[p], [outs[p], from_right[p].at[z]])

        for zz in range(m):
            across(p, zz).wait_send()

            @pl.when(z < zz)
            def _():
                right(p, zz).wait_send()

            @pl.when(z > zz)
            def _():
                left(p, zz).wait_send()


def scatter_dp(arrays, count, collective_id):
    pieces, m = len(arrays), count // 2
    dma = pltpu.SemaphoreType.DMA
    slots = [pltpu.VMEM((m,) + a.shape[1:], a.dtype) for a in arrays]
    vmem = pl.BlockSpec(memory_space=pltpu.VMEM)
    return pl.pallas_call(
        functools.partial(scatter_kernel, count, pieces),
        out_shape=[jax.ShapeDtypeStruct(a.shape[1:], jnp.float32) for a in arrays],
        in_specs=[vmem] * pieces,
        out_specs=[vmem] * pieces,
        scratch_shapes=slots * 4 + [dma((pieces, m))] * 5,
        compiler_params=pltpu.CompilerParams(
            collective_id=collective_id, has_side_effects=True, vmem_limit_bytes=40 * 2**20
        ),
        name="sum_to_owners",
    )(*arrays)


def merge_kernel(first, heads, away_ref, near_ref, mix, here, there, up, down, out):
    away = away_ref[pl.program_id(1)]
    rank = up.shape[-1]
    down_part = down[0][:, first : first + rank]

    def run(base):
        def step(h, carry):
            mixed_up = jnp.dot(mix[...], up[0, h], preferred_element_type=jnp.float32)
            product = lax.dot_general(
                mixed_up.astype(jnp.bfloat16),
                down_part,
                (((1,), (1,)), ((), ())),
                preferred_element_type=jnp.float32,
            )
            rows = jnp.dot(mix[...], base[0, h], preferred_element_type=jnp.float32)
            out[0, h] = (rows + adapter_scale * product).astype(jnp.bfloat16)
            return carry

        lax.fori_loop(0, heads, step, 0, unroll=True)

    @pl.when(away == 0)
    def _():
        run(here)

    @pl.when(away != 0)
    def _():
        run(there)


def merge(base_here, base_there, rank_up, rank_down, mix, away, near, first):
    layers, head_count, size, width = base_here.shape
    slots = away.shape[0]
    per_slot = head_count // slots
    heads = min(8, per_slot)
    steps = per_slot // heads
    rank = rank_up.shape[-1]

    def here_map(l, g, c, away, near):
        return jnp.where(away[g] == 0, l, 0), jnp.where(away[g] == 0, near[g] * steps + c, 0), 0, 0

    def there_map(l, g, c, away, near):
        return jnp.where(away[g] == 0, 0, l), jnp.where(away[g] == 0, 0, near[g] * steps + c), 0, 0

    def slot_map(l, g, c, away, near):
        return l, g * steps + c, 0, 0

    block = (1, heads, size, width)
    return pl.pallas_call(
        functools.partial(merge_kernel, first, heads),
        out_shape=jax.ShapeDtypeStruct(base_here.shape, base_here.dtype),
        grid_spec=pltpu.PrefetchScalarGridSpec(
            num_scalar_prefetch=2,
            grid=(layers, slots, steps),
            in_specs=[
                pl.BlockSpec((size, size), lambda l, g, c, away, near: (0, 0)),
                pl.BlockSpec(block, here_map),
                pl.BlockSpec(block, there_map),
                pl.BlockSpec((1, heads, size, rank), slot_map),
                pl.BlockSpec((1, width, rank_down.shape[-1]), lambda l, g, c, away, near: (l, 0, 0)),
            ],
            out_specs=pl.BlockSpec(block, slot_map),
        ),
        compiler_params=pltpu.CompilerParams(vmem_limit_bytes=40 * 2**20),
        name="merged_rows",
    )(away, near, mix, base_here, base_there, rank_up, rank_down)


def swap_core(value):
    return lax.ppermute(value, "tensor", [(0, 1), (1, 0)])


def body(
    acts,
    grad_query,
    keyvalue_gradient,
    attn_out,
    grad_out,
    seq_lengths,
    group_ids,
    rewards,
    wide_params,
    wide_moments,
    head_params,
    head_moments,
    key_value_adapters,
    kv_moments,
    base_query,
    frozen_key_rows,
    rotary_rows,
    rollout_group_order,
):
    count = lax.axis_size("dp")
    tensor_pos = lax.axis_index("tensor")
    layers, tokens, model_width = acts.shape
    wide_rows = wide_params.shape[1]
    rank = wide_params.shape[2] // 4
    heads, share_rows = head_params.shape[1:3]
    kv_heads = key_value_adapters.shape[1]
    all_heads = heads + kv_heads
    base_there = swap_core(base_query)
    frozen_there = swap_core(frozen_key_rows)

    wide_bf = wide_params.astype(jnp.bfloat16).reshape(-1, 4 * rank)
    head_bf = jnp.concatenate([head_params, key_value_adapters], axis=1).astype(jnp.bfloat16)
    wide_all, head_all = gather_dp([wide_bf, head_bf.reshape(-1, 2 * rank)], [], count, False, 0)
    wide_all = wide_all.reshape(count, layers, wide_rows, 4 * rank)
    head_all = head_all.reshape(count, layers, all_heads, share_rows, 2 * rank)
    head_all = head_all.transpose(1, 2, 0, 3, 4).reshape(layers, all_heads, -1, 2 * rank)

    def own_columns(value):
        split = value.reshape(layers, tokens, count, 2, wide_rows)
        return lax.dynamic_index_in_dim(split, tensor_pos, 3, keepdims=False).reshape(
            layers, tokens, count * wide_rows
        )

    x_own, out_own = own_columns(acts), own_columns(grad_out)
    weight_col = token_weights(seq_lengths, group_ids, rewards, tokens)[:, None]
    dot = functools.partial(jnp.dot, preferred_element_type=jnp.float32)
    parts = []
    for layer in range(layers):
        wide = wide_all[:, layer].reshape(-1, 4 * rank)
        flat_head = head_all[layer, :heads].reshape(-1, 2 * rank)
        flat_kv = head_all[layer, heads:].reshape(-1, 2 * rank)
        parts.append(
            jnp.concatenate(
                [
                    dot(x_own[layer], wide)[:, : 3 * rank],
                    dot(out_own[layer], wide)[:, 3 * rank :],
                    dot(grad_query[layer], flat_head)[:, :rank],
                    dot(attn_out[layer], flat_head)[:, rank:],
                    dot(keyvalue_gradient[layer, :, 0], flat_kv)[:, :rank],
                    dot(keyvalue_gradient[layer, :, 1], flat_kv)[:, rank:],
                ],
                axis=1,
            )
        )
    part = jnp.stack(parts)
    low = (weight_col * (part + swap_core(part))).astype(jnp.bfloat16)
    wide_chunks, head_chunks = [], []
    for layer in range(layers):
        hidden = low[layer, :, : 3 * rank]
        gate_output = low[layer, :, 3 * rank : 4 * rank]
        gate_query = low[layer, :, 4 * rank : 5 * rank]
        hidden_output = low[layer, :, 5 * rank : 6 * rank]
        gate_kv = low[layer, :, 6 * rank :]
        none = jnp.zeros((tokens, rank), jnp.bfloat16)
        wide_grad = contracted_rows(
            x_own[layer], jnp.concatenate([gate_query, gate_kv, none], axis=1)
        ) + contracted_rows(
            out_own[layer], jnp.concatenate([none, none, none, hidden_output], axis=1)
        )
        head_grad = contracted_rows(
            grad_query[layer], jnp.concatenate([hidden[:, :rank], none], axis=1)
        ) + contracted_rows(attn_out[layer], jnp.concatenate([none, gate_output], axis=1))
        kv_grad = contracted_rows(
            keyvalue_gradient[layer, :, 0],
            jnp.concatenate([hidden[:, rank : 2 * rank], none], axis=1),
        ) + contracted_rows(
            keyvalue_gradient[layer, :, 1],
            jnp.concatenate([none, hidden[:, 2 * rank :]], axis=1),
        )
        wide_chunks.append((adapter_scale * wide_grad).astype(jnp.bfloat16))
        head_chunks.append(
            jnp.concatenate(
                [
                    (adapter_scale * grad).astype(jnp.bfloat16).reshape(-1, count, share_rows, 2 * rank)
                    for grad in (head_grad, kv_grad)
                ]
            ).transpose(1, 0, 2, 3)
        )
    wide_send = jnp.stack(
        [chunk.reshape(count, wide_rows, 4 * rank) for chunk in wide_chunks], axis=1
    ).reshape(count, -1, 4 * rank)
    head_send = jnp.stack(head_chunks, axis=1).reshape(count, -1, 2 * rank)
    wide_sum, head_sum = scatter_dp([wide_send, head_send], count, 1)
    wide_grad = wide_sum.reshape(wide_params.shape)
    head_sum = head_sum.reshape(layers, all_heads, share_rows, 2 * rank)
    new_wide, new_wide_moments = adamw(wide_params, wide_moments, wide_grad)
    new_head, new_head_moments = adamw(head_params, head_moments, head_sum[:, :heads])
    new_kv, new_kv_moments = adamw(key_value_adapters, kv_moments, head_sum[:, heads:])

    up_own = jnp.concatenate([new_head[..., :rank], new_kv[..., :rank]], axis=1).astype(jnp.bfloat16)
    down_own = new_wide[..., : 2 * rank].astype(jnp.bfloat16)
    up_here, up_there, down_there = gather_dp(
        [up_own.reshape(-1, 2 * rank)], [down_own.reshape(-1, 2 * rank)], count, True, 2
    )
    down_there = down_there.reshape(down_own.shape)
    first = tensor_pos == 0
    rank_down = jnp.concatenate(
        [jnp.where(first, down_own, down_there), jnp.where(first, down_there, down_own)], axis=1
    )

    slot_groups = kv_heads
    group_slots = tensor_pos * slot_groups + jnp.arange(slot_groups, dtype=jnp.int32)
    source_groups = jnp.take(rollout_group_order, group_slots)
    away = (source_groups // slot_groups != tensor_pos).astype(jnp.int32)
    near = (source_groups % slot_groups).astype(jnp.int32)

    both = jnp.stack([up_here, up_there]).reshape(2, count, layers, all_heads, share_rows, rank)

    def picked(low_head, amount):
        grouped = both[:, :, :, low_head : low_head + amount].reshape(
            2, count, layers, slot_groups, amount // slot_groups, share_rows, rank
        )
        rows = [
            lax.dynamic_index_in_dim(
                lax.dynamic_index_in_dim(grouped, away[slot], 0, keepdims=False),
                near[slot],
                2,
                keepdims=False,
            )
            for slot in range(slot_groups)
        ]
        stacked = jnp.stack(rows, axis=2)
        return stacked.transpose(1, 2, 3, 0, 4, 5).reshape(layers, amount, -1, rank)

    mix = (rotary_rows[:, None] == jnp.arange(rotary_rows.shape[0], dtype=jnp.int32)[None, :]).astype(
        jnp.bfloat16
    )
    merged_query = merge(
        base_query, base_there, picked(0, heads), rank_down, mix, away, near, 0
    )
    merged_key = merge(
        frozen_key_rows, frozen_there, picked(heads, kv_heads), rank_down, mix, away, near, rank
    )
    return (
        new_wide,
        new_wide_moments,
        new_head,
        new_head_moments,
        new_kv,
        new_kv_moments,
        merged_query,
        merged_key,
    )


def solution(mesh):
    placed = (
        P("groups", "dp", None),
        P("groups", "dp", "tensor"),
        P("groups", "dp", None, "tensor"),
        P("groups", "dp", "tensor"),
        P("groups", "dp", None),
        P("dp", "groups"),
        P("dp", "groups"),
        P("dp", "groups"),
        P("groups", ("dp", "tensor"), None),
        P(None, "groups", ("dp", "tensor"), None),
        P("groups", "tensor", "dp", None),
        P(None, "groups", "tensor", "dp", None),
        P("groups", "tensor", "dp", None),
        P(None, "groups", "tensor", "dp", None),
        P(None, "tensor", None, "dp"),
        P(None, "tensor", None, "dp"),
        P(),
        P(),
    )
    return jax.shard_map(
        body,
        mesh=mesh,
        in_specs=placed,
        out_specs=(
            P("groups", ("dp", "tensor"), None),
            P(None, "groups", ("dp", "tensor"), None),
            P("groups", "tensor", "dp", None),
            P(None, "groups", "tensor", "dp", None),
            P("groups", "tensor", "dp", None),
            P(None, "groups", "tensor", "dp", None),
            P("groups", "tensor", None, "dp"),
            P("groups", "tensor", None, "dp"),
        ),
        check_vma=False,
    )
```

```python
import functools

import jax
import jax.numpy as jnp
from jax import lax
from jax.experimental import pallas as pl
from jax.experimental.pallas import tpu as pltpu
from jax.sharding import PartitionSpec as P

adapter_scale = 2.0
beta_one = 0.9
beta_two = 0.99
learn_rate = 0.002
decay_rate = 0.01
adam_eps = 1e-08
bias_one = 1.0 - beta_one**20
bias_two = 1.0 - beta_two**20


def token_weights(seq_lengths, group_ids, rewards, count):
    seq_ends = jnp.cumsum(seq_lengths, axis=-1)
    starts = seq_ends - seq_lengths
    places = jnp.arange(count, dtype=jnp.int32)
    member = (
        (places[None, :, None] >= starts[:, None, :])
        & (places[None, :, None] < seq_ends[:, None, :])
    ).astype(jnp.float32)
    same_group = (group_ids[:, :, None] == group_ids[:, None, :]).astype(jnp.float32)
    group_mean = jnp.sum(same_group * rewards[:, None, :], axis=-1) / jnp.sum(same_group, axis=-1)
    advantage = rewards - group_mean
    per_seq = advantage / seq_lengths.astype(jnp.float32)
    return jnp.sum(member * per_seq[:, None, :], axis=-1).reshape(-1)


def contracted_rows(left, right):
    return lax.dot_general(
        left, right, (((0,), (0,)), ((), ())), preferred_element_type=jnp.float32
    )


def adamw(parameter, moments, gradient):
    first_moment = beta_one * moments[0] + (1.0 - beta_one) * gradient
    second_moment = beta_two * moments[1] + (1.0 - beta_two) * gradient * gradient
    update = first_moment / bias_one / (jnp.sqrt(second_moment / bias_two) + adam_eps)
    return (
        parameter - learn_rate * (update + decay_rate * parameter),
        jnp.stack([first_moment, second_moment]),
    )


MESH = pl.DeviceIdType.MESH
ROW_STEP = 32


def remote(src, dst, send_sem, recv_sem, device):
    return pltpu.make_async_remote_copy(
        src_ref=src,
        dst_ref=dst,
        send_sem=send_sem,
        recv_sem=recv_sem,
        device_id=device,
        device_id_type=MESH,
    )


def place(count):
    me = lax.axis_index("dp")
    return me, me // 2, me % 2, count // 2


def greet(z, m, partners):
    me = lax.axis_index("dp")
    barrier = pltpu.get_barrier_semaphore()
    for device in partners:
        pl.semaphore_signal(barrier, inc=1, device_id=device, device_id_type=MESH)

    @pl.when(z > 0)
    def _():
        pl.semaphore_signal(barrier, inc=1, device_id={"dp": me - 2}, device_id_type=MESH)

    @pl.when(z < m - 1)
    def _():
        pl.semaphore_signal(barrier, inc=1, device_id={"dp": me + 2}, device_id_type=MESH)

    ends = jnp.where(z > 0, 1, 0) + jnp.where(z < m - 1, 1, 0)
    pl.semaphore_wait(barrier, len(partners) + ends)


def gather_kernel(count, pieces, share, swaps, *refs):
    refs = list(refs)
    take = lambda k: [refs.pop(0) for _ in range(k)]
    ins, swap_ins = take(pieces), take(swaps)
    outs, others, swap_outs = take(pieces), take(pieces if share else 0), take(swaps)
    send_right, send_left, send_row, recv, local_sem = take(5)
    send_core, recv_core = take(2) if share else (None, None)
    send_swap, recv_swap = take(2) if swaps else (None, None)
    sems = (send_right, send_left, send_row, recv, local_sem, send_core, recv_core, send_swap, recv_swap)
    exchange(count, ins, swap_ins, outs, others, swap_outs, sems, share, False, None)


def exchange(count, ins, swap_ins, outs, others, swap_outs, sems, share, greet_core, use):
    pieces, swaps = len(ins), len(swap_ins)
    (send_right, send_left, send_row, recv, local_sem, send_core, recv_core, send_swap, recv_swap) = sems
    use = use or (lambda p, slot: None)
    me, z, y, m = place(count)
    row_mate = {"dp": me + 1 - 2 * y}
    core_mate = {"tensor": 1 - lax.axis_index("tensor")}
    has_left, has_right = z > 0, z < m - 1
    greet(z, m, [row_mate] + ([core_mate] if share or swaps or greet_core else []))

    def right(p, src, k):
        slot = (z - k) * 2 + y
        return remote(src(slot), outs[p].at[slot], send_right.at[p, k], recv.at[p, slot], {"dp": me + 2})

    def left(p, src, k):
        slot = (z + k) * 2 + y
        return remote(src(slot), outs[p].at[slot], send_left.at[p, k], recv.at[p, slot], {"dp": me - 2})

    def across(p, src, zz):
        slot = zz * 2 + y
        return remote(src(slot), outs[p].at[slot], send_row.at[p, zz], recv.at[p, slot], row_mate)

    def to_core(p, src, slot):
        return remote(src(slot), others[p].at[slot], send_core.at[p, slot], recv_core.at[p, slot], core_mate)

    def arrive(p, slot):
        remote(outs[p].at[slot], outs[p].at[slot], send_row.at[p, 0], recv.at[p, slot], row_mate).wait_recv()

    own = [lambda slot, r=r: r for r in ins]
    held = [lambda slot, r=r: r.at[slot] for r in outs]

    for s in range(swaps):
        remote(swap_ins[s], swap_outs[s], send_swap.at[s], recv_swap.at[s], core_mate).start()
    for p in range(pieces):

        @pl.when(has_right)
        def _():
            right(p, own[p], 0).start()

        @pl.when(has_left)
        def _():
            left(p, own[p], 0).start()

        across(p, own[p], z).start()
        if share:
            to_core(p, own[p], me).start()
        pltpu.make_async_copy(ins[p], outs[p].at[me], local_sem.at[p]).start()
    for p in range(pieces):
        pltpu.make_async_copy(ins[p], outs[p].at[me], local_sem.at[p]).wait()
        use(p, me)

    for k in range(1, m):
        for p in range(pieces):

            @pl.when(z - k >= 0)
            def _():
                slot = (z - k) * 2 + y
                arrive(p, slot)

                @pl.when(has_right)
                def _():
                    right(p, held[p], k).start()

                across(p, held[p], z - k).start()
                if share:
                    to_core(p, held[p], slot).start()
                use(p, slot)

            @pl.when(z + k < m)
            def _():
                slot = (z + k) * 2 + y
                arrive(p, slot)

                @pl.when(has_left)
                def _():
                    left(p, held[p], k).start()

                across(p, held[p], z + k).start()
                if share:
                    to_core(p, held[p], slot).start()
                use(p, slot)

    far = 1 - y
    for zz in range(m):
        for p in range(pieces):
            slot = zz * 2 + far
            arrive(p, slot)
            if share:
                to_core(p, held[p], slot).start()
            use(p, slot)
    for p in range(pieces):
        for zz in range(m):
            across(p, held[p], zz).wait_send()
        for k in range(m):

            @pl.when(has_right & (z - k >= 0))
            def _():
                right(p, held[p], k).wait_send()

            @pl.when(has_left & (z + k < m))
            def _():
                left(p, held[p], k).wait_send()

        if share:
            for slot in range(count):
                to_core(p, held[p], slot).wait()
    for s in range(swaps):
        remote(swap_ins[s], swap_outs[s], send_swap.at[s], recv_swap.at[s], core_mate).wait()


def gather_dp(arrays, swapped, count, share, collective_id):
    pieces, swaps, m = len(arrays), len(swapped), count // 2
    stacked = [jax.ShapeDtypeStruct((count,) + a.shape, a.dtype) for a in arrays]
    dma = pltpu.SemaphoreType.DMA
    scratch = [dma((pieces, m)), dma((pieces, m)), dma((pieces, m)), dma((pieces, count)), dma((pieces,))]
    if share:
        scratch += [dma((pieces, count)), dma((pieces, count))]
    if swaps:
        scratch += [dma((swaps,)), dma((swaps,))]
    shapes = stacked + (stacked if share else []) + [
        jax.ShapeDtypeStruct(a.shape, a.dtype) for a in swapped
    ]
    anywhere = pl.BlockSpec(memory_space=pl.ANY)
    return pl.pallas_call(
        functools.partial(gather_kernel, count, pieces, share, swaps),
        out_shape=shapes,
        in_specs=[anywhere] * (pieces + swaps),
        out_specs=[anywhere] * len(shapes),
        scratch_shapes=scratch,
        compiler_params=pltpu.CompilerParams(collective_id=collective_id, has_side_effects=True),
        name="gather_pieces",
    )(*arrays, *swapped)


def column_copy(array, held, sems, slot, width):
    first = pl.multiple_of((slot * 2 + lax.axis_index("tensor")) * width, width)
    return pltpu.make_async_copy(array.at[:, :, pl.ds(first, width)], held.at[slot], sems.at[slot])


def product(left, right, contract=1):
    return lax.dot_general(
        left, right, (((contract,), (0,)), ((), ())), preferred_element_type=jnp.float32
    )


def forward_kernel(
    count,
    share_rows,
    wide_in,
    head_in,
    acts,
    grad_out,
    grad_query,
    attn_out,
    key_grad,
    value_grad,
    weights,
    out,
    wide_all,
    head_all,
    x_held,
    out_held,
    query_held,
    attn_held,
    x_total,
    out_total,
    query_total,
    attn_total,
    part,
    part_there,
    send_right,
    send_left,
    send_row,
    recv,
    local_sem,
    x_sem,
    out_sem,
    query_sem,
    attn_sem,
    core_send,
    core_recv,
):
    layers, tokens, _ = acts.shape
    width = wide_in.shape[0] // layers
    size = count * share_rows
    heads = grad_query.shape[2] // size
    all_heads = head_in.shape[0] // (layers * share_rows)
    core_mate = {"tensor": 1 - lax.axis_index("tensor")}
    for slot in range(count):
        column_copy(acts, x_held, x_sem, slot, width).start()
        column_copy(grad_out, out_held, out_sem, slot, width).start()
    for layer in range(layers):
        pltpu.make_async_copy(grad_query.at[layer], query_held.at[layer], query_sem.at[layer]).start()
        pltpu.make_async_copy(attn_out.at[layer], attn_held.at[layer], attn_sem.at[layer]).start()
    for total in (x_total, out_total, query_total, attn_total):
        total[...] = jnp.zeros_like(total)

    def use(p, slot):
        if p == 0:
            column_copy(acts, x_held, x_sem, slot, width).wait()
            column_copy(grad_out, out_held, out_sem, slot, width).wait()
            for layer in range(layers):
                factors = wide_all[slot, layer * width : (layer + 1) * width, :]
                x_total[layer] += product(x_held[slot, layer], factors)
                out_total[layer] += product(out_held[slot, layer], factors)

    sems = (send_right, send_left, send_row, recv, local_sem, None, None, None, None)
    exchange(count, [wide_in, head_in], [], [wide_all, head_all], [], [], sems, False, True, use)

    span = max(1, 16 // share_rows)

    def head_rows(layer, head):
        start = pl.multiple_of((layer * all_heads + head) * share_rows, span * share_rows)
        units = [head_all[slot, pl.ds(start, span * share_rows), :] for slot in range(count)]
        if span == 1:
            return jnp.concatenate(units, axis=0)
        units = [unit.astype(jnp.float32) for unit in units]
        rows = [unit[j * share_rows : (j + 1) * share_rows] for j in range(span) for unit in units]
        return jnp.concatenate(rows, axis=0).astype(head_all.dtype)

    half = head_in.shape[1]
    low_half = lax.broadcasted_iota(jnp.int32, (tokens, half), 1) < half // 2
    group = 4 if heads % 4 == 0 else 1

    def swap(layer):
        return remote(
            part.at[layer], part_there.at[layer], core_send.at[layer], core_recv.at[layer], core_mate
        )

    for layer in range(layers):
        pltpu.make_async_copy(grad_query.at[layer], query_held.at[layer], query_sem.at[layer]).wait()
        pltpu.make_async_copy(attn_out.at[layer], attn_held.at[layer], attn_sem.at[layer]).wait()

        def step(i, carry):
            factors = jnp.concatenate(
                [head_rows(layer, i * group + j) for j in range(0, group, span)], axis=0
            )
            columns = pl.ds(pl.multiple_of(i * group * size, group * size), group * size)
            query_total[layer] += product(query_held[layer, :, columns], factors)
            attn_total[layer] += product(attn_held[layer, :, columns], factors)
            return carry

        lax.fori_loop(0, heads // group, step, 0)
        kv_factors = jnp.concatenate(
            [head_rows(layer, heads + j) for j in range(0, all_heads - heads, span)], axis=0
        )
        part[layer, :, :half] = x_total[layer, :, :half]
        part[layer, :, half : 2 * half] = jnp.where(
            low_half, x_total[layer, :, half:], out_total[layer, :, half:]
        )
        part[layer, :, 2 * half : 3 * half] = jnp.where(
            low_half, query_total[layer], attn_total[layer]
        )
        part[layer, :, 3 * half :] = jnp.where(
            low_half, product(key_grad[layer], kv_factors), product(value_grad[layer], kv_factors)
        )
        swap(layer).start()

    for layer in range(layers):
        swap(layer).wait()

        def piece(k):
            columns = slice(k * half, (k + 1) * half)
            return weights[...] * (part[layer, :, columns] + part_there[layer, :, columns])

        hidden_qk, hidden_v_out, query_outer, key_value = (piece(k) for k in range(4))
        zero = jnp.zeros((tokens, half), jnp.float32)

        def turned(value):
            return pltpu.roll(value, half // 2, 1)

        columns = [
            jnp.where(low_half, query_outer, turned(key_value)),
            jnp.where(low_half, turned(key_value), zero),
            zero,
            jnp.where(low_half, zero, query_outer),
            jnp.where(low_half, hidden_qk, zero),
            jnp.where(low_half, zero, hidden_v_out),
            jnp.where(low_half, turned(hidden_qk), zero),
            jnp.where(low_half, zero, turned(hidden_v_out)),
        ]
        for k, value in enumerate(columns):
            out[layer, :, k * half : (k + 1) * half] = value.astype(jnp.bfloat16)


def forward(wide, head, acts, grad_out, grad_query, attn_out, key_grad, value_grad, weights, count, share_rows, collective_id):
    layers, tokens, _ = acts.shape
    width = wide.shape[0] // layers
    half = head.shape[1]
    m = count // 2
    dma = pltpu.SemaphoreType.DMA
    anywhere, vmem = pl.BlockSpec(memory_space=pl.ANY), pl.BlockSpec(memory_space=pltpu.VMEM)
    total = lambda columns: pltpu.VMEM((layers, tokens, columns), jnp.float32)
    return pl.pallas_call(
        functools.partial(forward_kernel, count, share_rows),
        out_shape=jax.ShapeDtypeStruct((layers, tokens, 8 * half), jnp.bfloat16),
        in_specs=[vmem] * 2 + [anywhere] * 4 + [vmem] * 3,
        out_specs=vmem,
        scratch_shapes=[
            pltpu.VMEM((count,) + wide.shape, wide.dtype),
            pltpu.VMEM((count,) + head.shape, head.dtype),
            pltpu.VMEM((count, layers, tokens, width), acts.dtype),
            pltpu.VMEM((count, layers, tokens, width), acts.dtype),
            pltpu.VMEM(grad_query.shape, grad_query.dtype),
            pltpu.VMEM(attn_out.shape, attn_out.dtype),
            total(2 * half),
            total(2 * half),
            total(half),
            total(half),
            total(4 * half),
            total(4 * half),
            dma((2, m)),
            dma((2, m)),
            dma((2, m)),
            dma((2, count)),
            dma((2,)),
            dma((count,)),
            dma((count,)),
            dma((layers,)),
            dma((layers,)),
            dma((layers,)),
            dma((layers,)),
        ],
        compiler_params=pltpu.CompilerParams(
            collective_id=collective_id, has_side_effects=True, vmem_limit_bytes=44 * 2**20
        ),
        name="gather_and_low_products",
    )(wide, head, acts, grad_out, grad_query, attn_out, key_grad, value_grad, weights)


def add_rows(dst, terms):
    def step(i, carry):
        rows = pl.ds(pl.multiple_of(i * ROW_STEP, ROW_STEP), ROW_STEP)
        total = terms[0][rows, :].astype(jnp.float32)
        for term in terms[1:]:
            total = total + term[rows, :].astype(jnp.float32)
        dst[rows, :] = total.astype(dst.dtype)
        return carry

    lax.fori_loop(0, dst.shape[0] // ROW_STEP, step, 0)


def backward_kernel(
    count,
    share_rows,
    acts,
    grad_out,
    grad_query,
    attn_out,
    key_grad,
    value_grad,
    low,
    wide_out,
    head_out,
    wide_mine,
    head_mine,
    x_held,
    out_held,
    query_held,
    attn_held,
    wide_row,
    head_row,
    wide_left,
    head_left,
    wide_right,
    head_right,
    wide_leaving,
    head_leaving,
    x_sem,
    out_sem,
    query_sem,
    attn_sem,
    row_send,
    row_recv,
    line_send,
    left_recv,
    right_recv,
):
    layers, tokens, _ = acts.shape
    width = wide_out.shape[0] // layers
    half = head_out.shape[1]
    size = count * share_rows
    heads = grad_query.shape[2] // size
    all_heads = head_out.shape[0] // (layers * share_rows)
    ins, outs = [wide_mine, head_mine], [wide_out, head_out]
    from_row, leaving = [wide_row, head_row], [wide_leaving, head_leaving]
    from_left, from_right = [wide_left, head_left], [wide_right, head_right]
    me, z, y, m = place(count)
    row_mate = {"dp": me + 1 - 2 * y}
    has_left, has_right = z > 0, z < m - 1

    def order(j):
        return jnp.where(2 * z < m, m - 1 - j, j)

    for j in range(m):
        for slot in (order(j) * 2 + 1 - y, order(j) * 2 + y):
            column_copy(acts, x_held, x_sem, slot, width).start()
            column_copy(grad_out, out_held, out_sem, slot, width).start()
    for layer in range(layers):
        pltpu.make_async_copy(grad_query.at[layer], query_held.at[layer], query_sem.at[layer]).start()
        pltpu.make_async_copy(attn_out.at[layer], attn_held.at[layer], attn_sem.at[layer]).start()

    def right_side(layer, first, amount):
        return low[layer, :, first * half : (first + amount) * half]

    def wide_chunk(slot):
        column_copy(acts, x_held, x_sem, slot, width).wait()
        column_copy(grad_out, out_held, out_sem, slot, width).wait()
        for layer in range(layers):
            grad = product(x_held[slot, layer], right_side(layer, 0, 2), 0) + product(
                out_held[slot, layer], right_side(layer, 2, 2), 0
            )
            wide_mine[slot, layer * width : (layer + 1) * width, :] = (adapter_scale * grad).astype(
                jnp.bfloat16
            )

    span = max(1, 16 // share_rows)

    def put_heads(layer, head, grad, amount):
        grad = adapter_scale * grad
        for j in range(0, amount, span):
            start = pl.multiple_of((layer * all_heads + head + j) * share_rows, span * share_rows)
            for slot in range(count):
                lows = [(j + i) * size + slot * share_rows for i in range(span)]
                rows = [grad[low_row : low_row + share_rows] for low_row in lows]
                rows = rows[0] if span == 1 else jnp.concatenate(rows, axis=0)
                head_mine[slot, pl.ds(start, span * share_rows), :] = rows.astype(jnp.bfloat16)

    def across(p, zz):
        return remote(
            ins[p].at[zz * 2 + 1 - y], from_row[p].at[zz], row_send.at[p, zz], row_recv.at[p, zz], row_mate
        )

    def right(p, zz):
        return remote(
            leaving[p].at[zz], from_left[p].at[zz], line_send.at[p, zz], left_recv.at[p, zz], {"dp": me + 2}
        )

    def left(p, zz):
        return remote(
            leaving[p].at[zz], from_right[p].at[zz], line_send.at[p, zz], right_recv.at[p, zz], {"dp": me - 2}
        )

    greet(z, m, [row_mate])
    for j in range(m):
        wide_chunk(order(j) * 2 + 1 - y)
        across(0, order(j)).start()

    group = 2 if heads % 2 == 0 else 1
    for layer in range(layers):
        pltpu.make_async_copy(grad_query.at[layer], query_held.at[layer], query_sem.at[layer]).wait()
        pltpu.make_async_copy(attn_out.at[layer], attn_held.at[layer], attn_sem.at[layer]).wait()

        def step(i, carry):
            columns = pl.ds(pl.multiple_of(i * group * size, group * size), group * size)
            grad = product(query_held[layer, :, columns], right_side(layer, 4, 1), 0) + product(
                attn_held[layer, :, columns], right_side(layer, 5, 1), 0
            )
            put_heads(layer, i * group, grad, group)
            return carry

        lax.fori_loop(0, heads // group, step, 0)
        kv = product(key_grad[layer], right_side(layer, 6, 1), 0) + product(
            value_grad[layer], right_side(layer, 7, 1), 0
        )
        put_heads(layer, heads, kv, all_heads - heads)

    for j in range(m):
        across(1, order(j)).start()
    for j in range(m):
        wide_chunk(order(j) * 2 + y)

    for p in range(2):
        for j in range(m):
            zz = order(j)

            @pl.when(zz > z)
            def _():
                across(p, zz).wait_recv()
                near = [ins[p].at[zz * 2 + y], from_row[p].at[zz]]

                @pl.when(has_left)
                def _():
                    right(p, zz).wait_recv()
                    add_rows(leaving[p].at[zz], near + [from_left[p].at[zz]])

                @pl.when(jnp.logical_not(has_left))
                def _():
                    add_rows(leaving[p].at[zz], near)

                right(p, zz).start()

            @pl.when(zz < z)
            def _():
                across(p, zz).wait_recv()
                near = [ins[p].at[zz * 2 + y], from_row[p].at[zz]]

                @pl.when(has_right)
                def _():
                    left(p, zz).wait_recv()
                    add_rows(leaving[p].at[zz], near + [from_right[p].at[zz]])

                @pl.when(jnp.logical_not(has_right))
                def _():
                    add_rows(leaving[p].at[zz], near)

                left(p, zz).start()

    for p in range(2):
        across(p, z).wait_recv()
        add_rows(outs[p], [ins[p].at[me], from_row[p].at[z]])

        @pl.when(has_left)
        def _():
            right(p, z).wait_recv()
            add_rows(outs[p], [outs[p], from_left[p].at[z]])

        @pl.when(has_right)
        def _():
            left(p, z).wait_recv()
            add_rows(outs[p], [outs[p], from_right[p].at[z]])

        for zz in range(m):
            across(p, zz).wait_send()

            @pl.when(z < zz)
            def _():
                right(p, zz).wait_send()

            @pl.when(z > zz)
            def _():
                left(p, zz).wait_send()


def backward(acts, grad_out, grad_query, attn_out, key_grad, value_grad, low, width, all_heads, share_rows, count, collective_id):
    layers, tokens, _ = acts.shape
    half, m = low.shape[2] // 8, count // 2
    dma = pltpu.SemaphoreType.DMA
    anywhere, vmem = pl.BlockSpec(memory_space=pl.ANY), pl.BlockSpec(memory_space=pltpu.VMEM)
    wide = (layers * width, 2 * half)
    head = (layers * all_heads * share_rows, half)
    slots = [pltpu.VMEM((m,) + shape, jnp.bfloat16) for shape in (wide, head)]
    return pl.pallas_call(
        functools.partial(backward_kernel, count, share_rows),
        out_shape=[jax.ShapeDtypeStruct(shape, jnp.float32) for shape in (wide, head)],
        in_specs=[anywhere] * 4 + [vmem] * 3,
        out_specs=[vmem] * 2,
        scratch_shapes=[pltpu.VMEM((count,) + shape, jnp.bfloat16) for shape in (wide, head)]
        + [
            pltpu.VMEM((count, layers, tokens, width), acts.dtype),
            pltpu.VMEM((count, layers, tokens, width), acts.dtype),
            pltpu.VMEM(grad_query.shape, grad_query.dtype),
            pltpu.VMEM(attn_out.shape, attn_out.dtype),
        ]
        + slots * 4
        + [dma((count,)), dma((count,)), dma((layers,)), dma((layers,))]
        + [dma((2, m))] * 5,
        compiler_params=pltpu.CompilerParams(
            collective_id=collective_id, has_side_effects=True, vmem_limit_bytes=48 * 2**20
        ),
        name="gradients_to_owners",
    )(acts, grad_out, grad_query, attn_out, key_grad, value_grad, low)


def merge_kernel(first, heads, away_ref, near_ref, mix, here, there, up, down, out):
    away = away_ref[pl.program_id(1)]
    rank = up.shape[-1]
    down_part = down[0, first : first + rank, :]

    def run(base):
        def step(h, carry):
            mixed_up = (adapter_scale * product(mix[...], up[0, 0, h])).astype(jnp.bfloat16)
            left = jnp.concatenate([mix[...], mixed_up], axis=1)
            right = jnp.concatenate([base[0, h], down_part], axis=0)
            out[0, h] = product(left, right).astype(jnp.bfloat16)
            return carry

        lax.fori_loop(0, heads, step, 0, unroll=True)

    @pl.when(away == 0)
    def _():
        run(here)

    @pl.when(away != 0)
    def _():
        run(there)


def merge(base_here, base_there, rank_up, rank_down, mix, away, near, first, low_head):
    layers, head_count, size, width = base_here.shape
    slots = away.shape[0]
    per_slot = head_count // slots
    heads = min(8, per_slot)
    steps = per_slot // heads
    rank = rank_up.shape[-1]

    def here_map(l, g, c, away, near):
        return jnp.where(away[g] == 0, l, 0), jnp.where(away[g] == 0, near[g] * steps + c, 0), 0, 0

    def there_map(l, g, c, away, near):
        return jnp.where(away[g] == 0, 0, l), jnp.where(away[g] == 0, 0, near[g] * steps + c), 0, 0

    def slot_map(l, g, c, away, near):
        return l, g * steps + c, 0, 0

    def up_map(l, g, c, away, near):
        return away[g], l, low_head // heads + near[g] * steps + c, 0, 0

    block = (1, heads, size, width)
    return pl.pallas_call(
        functools.partial(merge_kernel, first, heads),
        out_shape=jax.ShapeDtypeStruct(base_here.shape, base_here.dtype),
        grid_spec=pltpu.PrefetchScalarGridSpec(
            num_scalar_prefetch=2,
            grid=(layers, slots, steps),
            in_specs=[
                pl.BlockSpec((size, size), lambda l, g, c, away, near: (0, 0)),
                pl.BlockSpec(block, here_map),
                pl.BlockSpec(block, there_map),
                pl.BlockSpec((1, 1, heads, size, rank), up_map),
                pl.BlockSpec((1, rank_down.shape[1], width), lambda l, g, c, away, near: (l, 0, 0)),
            ],
            out_specs=pl.BlockSpec(block, slot_map),
        ),
        compiler_params=pltpu.CompilerParams(vmem_limit_bytes=40 * 2**20),
        name="merged_rows",
    )(away, near, mix, base_here, base_there, rank_up, rank_down)


def swap_core(value):
    return lax.ppermute(value, "tensor", [(0, 1), (1, 0)])


def body(
    acts,
    grad_query,
    keyvalue_gradient,
    attn_out,
    grad_out,
    seq_lengths,
    group_ids,
    rewards,
    wide_params,
    wide_moments,
    head_params,
    head_moments,
    key_value_adapters,
    kv_moments,
    base_query,
    frozen_key_rows,
    rotary_rows,
    rollout_group_order,
):
    count = lax.axis_size("dp")
    tensor_pos = lax.axis_index("tensor")
    layers, tokens, model_width = acts.shape
    wide_rows = wide_params.shape[1]
    rank = wide_params.shape[2] // 4
    heads, share_rows = head_params.shape[1:3]
    kv_heads = key_value_adapters.shape[1]
    all_heads = heads + kv_heads
    base_there = swap_core(base_query)
    frozen_there = swap_core(frozen_key_rows)

    wide_bf = wide_params.astype(jnp.bfloat16).reshape(-1, 4 * rank)
    head_bf = jnp.concatenate([head_params, key_value_adapters], axis=1).astype(jnp.bfloat16)
    weight_col = token_weights(seq_lengths, group_ids, rewards, tokens)[:, None]
    key_grad, value_grad = keyvalue_gradient[:, :, 0], keyvalue_gradient[:, :, 1]
    rows = (acts, grad_out, grad_query, attn_out, key_grad, value_grad)
    low = forward(
        wide_bf, head_bf.reshape(-1, 2 * rank), *rows, weight_col, count, share_rows, 0
    )
    wide_sum, head_sum = backward(*rows, low, wide_rows, all_heads, share_rows, count, 1)
    wide_grad = wide_sum.reshape(wide_params.shape)
    head_sum = head_sum.reshape(layers, all_heads, share_rows, 2 * rank)
    new_wide, new_wide_moments = adamw(wide_params, wide_moments, wide_grad)
    new_head, new_head_moments = adamw(head_params, head_moments, head_sum[:, :heads])
    new_kv, new_kv_moments = adamw(key_value_adapters, kv_moments, head_sum[:, heads:])

    up_own = jnp.concatenate([new_head[..., :rank], new_kv[..., :rank]], axis=1).astype(jnp.bfloat16)
    down_own = new_wide[..., : 2 * rank].astype(jnp.bfloat16)
    up_here, up_there, down_there = gather_dp(
        [up_own.reshape(-1, 2 * rank)], [down_own.reshape(-1, 2 * rank)], count, True, 2
    )
    down_there = down_there.reshape(down_own.shape)
    first = tensor_pos == 0
    rank_down = jnp.concatenate(
        [jnp.where(first, down_own, down_there), jnp.where(first, down_there, down_own)], axis=1
    ).transpose(0, 2, 1)

    slot_groups = kv_heads
    group_slots = tensor_pos * slot_groups + jnp.arange(slot_groups, dtype=jnp.int32)
    source_groups = jnp.take(rollout_group_order, group_slots)
    away = (source_groups // slot_groups != tensor_pos).astype(jnp.int32)
    near = (source_groups % slot_groups).astype(jnp.int32)

    both = jnp.stack([up_here, up_there]).reshape(2, count, layers, all_heads, share_rows, rank)
    both = both.transpose(0, 2, 3, 1, 4, 5).reshape(2, layers, all_heads, -1, rank)
    mix = (rotary_rows[:, None] == jnp.arange(rotary_rows.shape[0], dtype=jnp.int32)[None, :]).astype(
        jnp.bfloat16
    )
    merged_query = merge(
        base_query, base_there, both, rank_down, mix, away, near, 0, 0
    )
    merged_key = merge(
        frozen_key_rows, frozen_there, both, rank_down, mix, away, near, rank, heads
    )
    return (
        new_wide,
        new_wide_moments,
        new_head,
        new_head_moments,
        new_kv,
        new_kv_moments,
        merged_query,
        merged_key,
    )


def solution(mesh):
    placed = (
        P("groups", "dp", None),
        P("groups", "dp", "tensor"),
        P("groups", "dp", None, "tensor"),
        P("groups", "dp", "tensor"),
        P("groups", "dp", None),
        P("dp", "groups"),
        P("dp", "groups"),
        P("dp", "groups"),
        P("groups", ("dp", "tensor"), None),
        P(None, "groups", ("dp", "tensor"), None),
        P("groups", "tensor", "dp", None),
        P(None, "groups", "tensor", "dp", None),
        P("groups", "tensor", "dp", None),
        P(None, "groups", "tensor", "dp", None),
        P(None, "tensor", None, "dp"),
        P(None, "tensor", None, "dp"),
        P(),
        P(),
    )
    return jax.shard_map(
        body,
        mesh=mesh,
        in_specs=placed,
        out_specs=(
            P("groups", ("dp", "tensor"), None),
            P(None, "groups", ("dp", "tensor"), None),
            P("groups", "tensor", "dp", None),
            P(None, "groups", "tensor", "dp", None),
            P("groups", "tensor", "dp", None),
            P(None, "groups", "tensor", "dp", None),
            P("groups", "tensor", None, "dp"),
            P("groups", "tensor", None, "dp"),
        ),
        check_vma=False,
    )
```

```python
import functools

import jax
import jax.numpy as jnp
from jax import lax
from jax.experimental import pallas as pl
from jax.experimental.pallas import tpu as pltpu
from jax.sharding import PartitionSpec as P

adapter_scale = 2.0
beta_one = 0.9
beta_two = 0.99
learn_rate = 0.002
decay_rate = 0.01
adam_eps = 1e-08
bias_one = 1.0 - beta_one**20
bias_two = 1.0 - beta_two**20


def token_weights(seq_lengths, group_ids, rewards, count):
    seq_ends = jnp.cumsum(seq_lengths, axis=-1)
    starts = seq_ends - seq_lengths
    places = jnp.arange(count, dtype=jnp.int32)
    member = (
        (places[None, :, None] >= starts[:, None, :])
        & (places[None, :, None] < seq_ends[:, None, :])
    ).astype(jnp.float32)
    same_group = (group_ids[:, :, None] == group_ids[:, None, :]).astype(jnp.float32)
    group_mean = jnp.sum(same_group * rewards[:, None, :], axis=-1) / jnp.sum(same_group, axis=-1)
    advantage = rewards - group_mean
    per_seq = advantage / seq_lengths.astype(jnp.float32)
    return jnp.sum(member * per_seq[:, None, :], axis=-1).reshape(-1)


def contracted_rows(left, right):
    return lax.dot_general(
        left, right, (((0,), (0,)), ((), ())), preferred_element_type=jnp.float32
    )


def adamw(parameter, moments, gradient):
    first_moment = beta_one * moments[0] + (1.0 - beta_one) * gradient
    second_moment = beta_two * moments[1] + (1.0 - beta_two) * gradient * gradient
    update = first_moment / bias_one / (jnp.sqrt(second_moment / bias_two) + adam_eps)
    return (
        parameter - learn_rate * (update + decay_rate * parameter),
        jnp.stack([first_moment, second_moment]),
    )


MESH = pl.DeviceIdType.MESH
ROW_STEP = 32


def remote(src, dst, send_sem, recv_sem, device):
    return pltpu.make_async_remote_copy(
        src_ref=src,
        dst_ref=dst,
        send_sem=send_sem,
        recv_sem=recv_sem,
        device_id=device,
        device_id_type=MESH,
    )


def place(count):
    me = lax.axis_index("dp")
    return me, me // 2, me % 2, count // 2


def greet(z, m, partners):
    me = lax.axis_index("dp")
    barrier = pltpu.get_barrier_semaphore()
    for device in partners:
        pl.semaphore_signal(barrier, inc=1, device_id=device, device_id_type=MESH)

    @pl.when(z > 0)
    def _():
        pl.semaphore_signal(barrier, inc=1, device_id={"dp": me - 2}, device_id_type=MESH)

    @pl.when(z < m - 1)
    def _():
        pl.semaphore_signal(barrier, inc=1, device_id={"dp": me + 2}, device_id_type=MESH)

    ends = jnp.where(z > 0, 1, 0) + jnp.where(z < m - 1, 1, 0)
    pl.semaphore_wait(barrier, len(partners) + ends)


def gather_kernel(count, pieces, share, swaps, *refs):
    refs = list(refs)
    take = lambda k: [refs.pop(0) for _ in range(k)]
    ins, swap_ins = take(pieces), take(swaps)
    outs, others, swap_outs = take(pieces), take(pieces if share else 0), take(swaps)
    send_right, send_left, send_row, recv, local_sem = take(5)
    send_core, recv_core = take(2) if share else (None, None)
    send_swap, recv_swap = take(2) if swaps else (None, None)
    sems = (send_right, send_left, send_row, recv, local_sem, send_core, recv_core, send_swap, recv_swap)
    exchange(count, ins, swap_ins, outs, others, swap_outs, sems, share, False, None)


def exchange(count, ins, swap_ins, outs, others, swap_outs, sems, share, greet_core, use):
    pieces, swaps = len(ins), len(swap_ins)
    (send_right, send_left, send_row, recv, local_sem, send_core, recv_core, send_swap, recv_swap) = sems
    use = use or (lambda p, slot: None)
    me, z, y, m = place(count)
    row_mate = {"dp": me + 1 - 2 * y}
    core_mate = {"tensor": 1 - lax.axis_index("tensor")}
    has_left, has_right = z > 0, z < m - 1
    greet(z, m, [row_mate] + ([core_mate] if share or swaps or greet_core else []))

    def right(p, src, k):
        slot = (z - k) * 2 + y
        return remote(src(slot), outs[p].at[slot], send_right.at[p, k], recv.at[p, slot], {"dp": me + 2})

    def left(p, src, k):
        slot = (z + k) * 2 + y
        return remote(src(slot), outs[p].at[slot], send_left.at[p, k], recv.at[p, slot], {"dp": me - 2})

    def across(p, src, zz):
        slot = zz * 2 + y
        return remote(src(slot), outs[p].at[slot], send_row.at[p, zz], recv.at[p, slot], row_mate)

    def to_core(p, src, slot):
        return remote(src(slot), others[p].at[slot], send_core.at[p, slot], recv_core.at[p, slot], core_mate)

    def arrive(p, slot):
        remote(outs[p].at[slot], outs[p].at[slot], send_row.at[p, 0], recv.at[p, slot], row_mate).wait_recv()

    own = [lambda slot, r=r: r for r in ins]
    held = [lambda slot, r=r: r.at[slot] for r in outs]

    for s in range(swaps):
        remote(swap_ins[s], swap_outs[s], send_swap.at[s], recv_swap.at[s], core_mate).start()
    for p in range(pieces):

        @pl.when(has_right)
        def _():
            right(p, own[p], 0).start()

        @pl.when(has_left)
        def _():
            left(p, own[p], 0).start()

        across(p, own[p], z).start()
        if share:
            to_core(p, own[p], me).start()
        pltpu.make_async_copy(ins[p], outs[p].at[me], local_sem.at[p]).start()
    for p in range(pieces):
        pltpu.make_async_copy(ins[p], outs[p].at[me], local_sem.at[p]).wait()
        use(p, me)

    for k in range(1, m):
        for p in range(pieces):

            @pl.when(z - k >= 0)
            def _():
                slot = (z - k) * 2 + y
                arrive(p, slot)

                @pl.when(has_right)
                def _():
                    right(p, held[p], k).start()

                across(p, held[p], z - k).start()
                if share:
                    to_core(p, held[p], slot).start()
                use(p, slot)

            @pl.when(z + k < m)
            def _():
                slot = (z + k) * 2 + y
                arrive(p, slot)

                @pl.when(has_left)
                def _():
                    left(p, held[p], k).start()

                across(p, held[p], z + k).start()
                if share:
                    to_core(p, held[p], slot).start()
                use(p, slot)

    far = 1 - y
    for zz in range(m):
        for p in range(pieces):
            slot = zz * 2 + far
            arrive(p, slot)
            if share:
                to_core(p, held[p], slot).start()
            use(p, slot)
    for p in range(pieces):
        for zz in range(m):
            across(p, held[p], zz).wait_send()
        for k in range(m):

            @pl.when(has_right & (z - k >= 0))
            def _():
                right(p, held[p], k).wait_send()

            @pl.when(has_left & (z + k < m))
            def _():
                left(p, held[p], k).wait_send()

        if share:
            for slot in range(count):
                to_core(p, held[p], slot).wait()
    for s in range(swaps):
        remote(swap_ins[s], swap_outs[s], send_swap.at[s], recv_swap.at[s], core_mate).wait()


def gather_dp(arrays, swapped, count, share, collective_id):
    pieces, swaps, m = len(arrays), len(swapped), count // 2
    stacked = [jax.ShapeDtypeStruct((count,) + a.shape, a.dtype) for a in arrays]
    dma = pltpu.SemaphoreType.DMA
    scratch = [dma((pieces, m)), dma((pieces, m)), dma((pieces, m)), dma((pieces, count)), dma((pieces,))]
    if share:
        scratch += [dma((pieces, count)), dma((pieces, count))]
    if swaps:
        scratch += [dma((swaps,)), dma((swaps,))]
    shapes = stacked + (stacked if share else []) + [
        jax.ShapeDtypeStruct(a.shape, a.dtype) for a in swapped
    ]
    anywhere = pl.BlockSpec(memory_space=pl.ANY)
    return pl.pallas_call(
        functools.partial(gather_kernel, count, pieces, share, swaps),
        out_shape=shapes,
        in_specs=[anywhere] * (pieces + swaps),
        out_specs=[anywhere] * len(shapes),
        scratch_shapes=scratch,
        compiler_params=pltpu.CompilerParams(collective_id=collective_id, has_side_effects=True),
        name="gather_pieces",
    )(*arrays, *swapped)


def column_copy(array, held, sems, slot, width):
    first = pl.multiple_of((slot * 2 + lax.axis_index("tensor")) * width, width)
    return pltpu.make_async_copy(array.at[:, :, pl.ds(first, width)], held.at[slot], sems.at[slot])


def product(left, right, contract=1):
    return lax.dot_general(
        left, right, (((contract,), (0,)), ((), ())), preferred_element_type=jnp.float32
    )


def forward_kernel(
    count,
    share_rows,
    wide_in,
    head_in,
    acts,
    grad_out,
    grad_query,
    attn_out,
    key_grad,
    value_grad,
    weights,
    out,
    wide_all,
    head_all,
    x_held,
    out_held,
    query_held,
    attn_held,
    x_total,
    out_total,
    query_total,
    attn_total,
    part,
    part_there,
    send_right,
    send_left,
    send_row,
    recv,
    local_sem,
    x_sem,
    out_sem,
    query_sem,
    attn_sem,
    core_send,
    core_recv,
):
    layers, tokens, _ = acts.shape
    width = wide_in.shape[0] // layers
    size = count * share_rows
    heads = grad_query.shape[2] // size
    all_heads = head_in.shape[0] // (layers * share_rows)
    core_mate = {"tensor": 1 - lax.axis_index("tensor")}
    for slot in range(count):
        column_copy(acts, x_held, x_sem, slot, width).start()
        column_copy(grad_out, out_held, out_sem, slot, width).start()
    for layer in range(layers):
        pltpu.make_async_copy(grad_query.at[layer], query_held.at[layer], query_sem.at[layer]).start()
        pltpu.make_async_copy(attn_out.at[layer], attn_held.at[layer], attn_sem.at[layer]).start()
    for total in (x_total, out_total, query_total, attn_total):
        total[...] = jnp.zeros_like(total)

    def use(p, slot):
        if p == 0:
            column_copy(acts, x_held, x_sem, slot, width).wait()
            column_copy(grad_out, out_held, out_sem, slot, width).wait()
            for layer in range(layers):
                factors = wide_all[slot, layer * width : (layer + 1) * width, :]
                x_total[layer] += product(x_held[slot, layer], factors)
                out_total[layer] += product(out_held[slot, layer], factors)

    sems = (send_right, send_left, send_row, recv, local_sem, None, None, None, None)
    exchange(count, [wide_in, head_in], [], [wide_all, head_all], [], [], sems, False, True, use)

    span = max(1, 16 // share_rows)

    def head_rows(layer, head):
        start = pl.multiple_of((layer * all_heads + head) * share_rows, span * share_rows)
        units = [head_all[slot, pl.ds(start, span * share_rows), :] for slot in range(count)]
        if span == 1:
            return jnp.concatenate(units, axis=0)
        units = [unit.astype(jnp.float32) for unit in units]
        rows = [unit[j * share_rows : (j + 1) * share_rows] for j in range(span) for unit in units]
        return jnp.concatenate(rows, axis=0).astype(head_all.dtype)

    half = head_in.shape[1]
    low_half = lax.broadcasted_iota(jnp.int32, (tokens, half), 1) < half // 2
    group = 4 if heads % 4 == 0 else 1

    def swap(layer):
        return remote(
            part.at[layer], part_there.at[layer], core_send.at[layer], core_recv.at[layer], core_mate
        )

    for layer in range(layers):
        pltpu.make_async_copy(grad_query.at[layer], query_held.at[layer], query_sem.at[layer]).wait()
        pltpu.make_async_copy(attn_out.at[layer], attn_held.at[layer], attn_sem.at[layer]).wait()

        def step(i, carry):
            factors = jnp.concatenate(
                [head_rows(layer, i * group + j) for j in range(0, group, span)], axis=0
            )
            columns = pl.ds(pl.multiple_of(i * group * size, group * size), group * size)
            query_total[layer] += product(query_held[layer, :, columns], factors)
            attn_total[layer] += product(attn_held[layer, :, columns], factors)
            return carry

        lax.fori_loop(0, heads // group, step, 0)
        kv_factors = jnp.concatenate(
            [head_rows(layer, heads + j) for j in range(0, all_heads - heads, span)], axis=0
        )
        part[layer, :, :half] = x_total[layer, :, :half]
        part[layer, :, half : 2 * half] = jnp.where(
            low_half, x_total[layer, :, half:], out_total[layer, :, half:]
        )
        part[layer, :, 2 * half : 3 * half] = jnp.where(
            low_half, query_total[layer], attn_total[layer]
        )
        part[layer, :, 3 * half :] = jnp.where(
            low_half, product(key_grad[layer], kv_factors), product(value_grad[layer], kv_factors)
        )
        swap(layer).start()

    for layer in range(layers):
        swap(layer).wait()

        def piece(k):
            columns = slice(k * half, (k + 1) * half)
            return weights[...] * (part[layer, :, columns] + part_there[layer, :, columns])

        hidden_qk, hidden_v_out, query_outer, key_value = (piece(k) for k in range(4))
        zero = jnp.zeros((tokens, half), jnp.float32)

        def turned(value):
            return pltpu.roll(value, half // 2, 1)

        columns = [
            jnp.where(low_half, query_outer, turned(key_value)),
            jnp.where(low_half, turned(key_value), zero),
            zero,
            jnp.where(low_half, zero, query_outer),
            jnp.where(low_half, hidden_qk, zero),
            jnp.where(low_half, zero, hidden_v_out),
            jnp.where(low_half, turned(hidden_qk), zero),
            jnp.where(low_half, zero, turned(hidden_v_out)),
        ]
        for k, value in enumerate(columns):
            out[layer, :, k * half : (k + 1) * half] = value.astype(jnp.bfloat16)


def forward(wide, head, acts, grad_out, grad_query, attn_out, key_grad, value_grad, weights, count, share_rows, collective_id):
    layers, tokens, _ = acts.shape
    width = wide.shape[0] // layers
    half = head.shape[1]
    m = count // 2
    dma = pltpu.SemaphoreType.DMA
    anywhere, vmem = pl.BlockSpec(memory_space=pl.ANY), pl.BlockSpec(memory_space=pltpu.VMEM)
    total = lambda columns: pltpu.VMEM((layers, tokens, columns), jnp.float32)
    return pl.pallas_call(
        functools.partial(forward_kernel, count, share_rows),
        out_shape=jax.ShapeDtypeStruct((layers, tokens, 8 * half), jnp.bfloat16),
        in_specs=[vmem] * 2 + [anywhere] * 4 + [vmem] * 3,
        out_specs=vmem,
        scratch_shapes=[
            pltpu.VMEM((count,) + wide.shape, wide.dtype),
            pltpu.VMEM((count,) + head.shape, head.dtype),
            pltpu.VMEM((count, layers, tokens, width), acts.dtype),
            pltpu.VMEM((count, layers, tokens, width), acts.dtype),
            pltpu.VMEM(grad_query.shape, grad_query.dtype),
            pltpu.VMEM(attn_out.shape, attn_out.dtype),
            total(2 * half),
            total(2 * half),
            total(half),
            total(half),
            total(4 * half),
            total(4 * half),
            dma((2, m)),
            dma((2, m)),
            dma((2, m)),
            dma((2, count)),
            dma((2,)),
            dma((count,)),
            dma((count,)),
            dma((layers,)),
            dma((layers,)),
            dma((layers,)),
            dma((layers,)),
        ],
        compiler_params=pltpu.CompilerParams(
            collective_id=collective_id, has_side_effects=True, vmem_limit_bytes=44 * 2**20
        ),
        name="gather_and_low_products",
    )(wide, head, acts, grad_out, grad_query, attn_out, key_grad, value_grad, weights)


def add_rows(dst, terms):
    def step(i, carry):
        rows = pl.ds(pl.multiple_of(i * ROW_STEP, ROW_STEP), ROW_STEP)
        total = terms[0][rows, :].astype(jnp.float32)
        for term in terms[1:]:
            total = total + term[rows, :].astype(jnp.float32)
        dst[rows, :] = total.astype(dst.dtype)
        return carry

    lax.fori_loop(0, dst.shape[0] // ROW_STEP, step, 0)


def backward_kernel(
    count,
    share_rows,
    acts,
    grad_out,
    grad_query,
    attn_out,
    key_grad,
    value_grad,
    low,
    wide_out,
    head_out,
    wide_mine,
    head_mine,
    x_held,
    out_held,
    query_held,
    attn_held,
    wide_row,
    head_row,
    wide_left,
    head_left,
    wide_right,
    head_right,
    wide_leaving,
    head_leaving,
    x_sem,
    out_sem,
    query_sem,
    attn_sem,
    row_send,
    row_recv,
    line_send,
    left_recv,
    right_recv,
):
    layers, tokens, _ = acts.shape
    width = wide_out.shape[0] // layers
    half = head_out.shape[1]
    size = count * share_rows
    heads = grad_query.shape[2] // size
    all_heads = head_out.shape[0] // (layers * share_rows)
    ins, outs = [wide_mine, head_mine], [wide_out, head_out]
    from_row, leaving = [wide_row, head_row], [wide_leaving, head_leaving]
    from_left, from_right = [wide_left, head_left], [wide_right, head_right]
    me, z, y, m = place(count)
    row_mate = {"dp": me + 1 - 2 * y}
    has_left, has_right = z > 0, z < m - 1

    def order(j):
        return jnp.where(2 * z < m, m - 1 - j, j)

    for j in range(m):
        for slot in (order(j) * 2 + 1 - y, order(j) * 2 + y):
            column_copy(acts, x_held, x_sem, slot, width).start()
            column_copy(grad_out, out_held, out_sem, slot, width).start()
    for layer in range(layers):
        pltpu.make_async_copy(grad_query.at[layer], query_held.at[layer], query_sem.at[layer]).start()
        pltpu.make_async_copy(attn_out.at[layer], attn_held.at[layer], attn_sem.at[layer]).start()

    def right_side(layer, first, amount):
        return low[layer, :, first * half : (first + amount) * half]

    def wide_chunk(slot):
        column_copy(acts, x_held, x_sem, slot, width).wait()
        column_copy(grad_out, out_held, out_sem, slot, width).wait()
        for layer in range(layers):
            grad = product(x_held[slot, layer], right_side(layer, 0, 2), 0) + product(
                out_held[slot, layer], right_side(layer, 2, 2), 0
            )
            wide_mine[slot, layer * width : (layer + 1) * width, :] = (adapter_scale * grad).astype(
                jnp.bfloat16
            )

    span = max(1, 16 // share_rows)

    def put_heads(layer, head, grad, amount):
        grad = adapter_scale * grad
        for j in range(0, amount, span):
            start = pl.multiple_of((layer * all_heads + head + j) * share_rows, span * share_rows)
            for slot in range(count):
                lows = [(j + i) * size + slot * share_rows for i in range(span)]
                rows = [grad[low_row : low_row + share_rows] for low_row in lows]
                rows = rows[0] if span == 1 else jnp.concatenate(rows, axis=0)
                head_mine[slot, pl.ds(start, span * share_rows), :] = rows.astype(jnp.bfloat16)

    def across(p, zz):
        return remote(
            ins[p].at[zz * 2 + 1 - y], from_row[p].at[zz], row_send.at[p, zz], row_recv.at[p, zz], row_mate
        )

    def right(p, zz):
        return remote(
            leaving[p].at[zz], from_left[p].at[zz], line_send.at[p, zz], left_recv.at[p, zz], {"dp": me + 2}
        )

    def left(p, zz):
        return remote(
            leaving[p].at[zz], from_right[p].at[zz], line_send.at[p, zz], right_recv.at[p, zz], {"dp": me - 2}
        )

    greet(z, m, [row_mate])
    for j in range(m):
        wide_chunk(order(j) * 2 + 1 - y)
        across(0, order(j)).start()

    group = 2 if heads % 2 == 0 else 1
    for layer in range(layers):
        pltpu.make_async_copy(grad_query.at[layer], query_held.at[layer], query_sem.at[layer]).wait()
        pltpu.make_async_copy(attn_out.at[layer], attn_held.at[layer], attn_sem.at[layer]).wait()

        def step(i, carry):
            columns = pl.ds(pl.multiple_of(i * group * size, group * size), group * size)
            grad = product(query_held[layer, :, columns], right_side(layer, 4, 1), 0) + product(
                attn_held[layer, :, columns], right_side(layer, 5, 1), 0
            )
            put_heads(layer, i * group, grad, group)
            return carry

        lax.fori_loop(0, heads // group, step, 0)
        kv = product(key_grad[layer], right_side(layer, 6, 1), 0) + product(
            value_grad[layer], right_side(layer, 7, 1), 0
        )
        put_heads(layer, heads, kv, all_heads - heads)

    for j in range(m):
        across(1, order(j)).start()
    for j in range(m):
        wide_chunk(order(j) * 2 + y)

    for p in range(2):
        for j in range(m):
            zz = order(j)

            @pl.when(zz > z)
            def _():
                across(p, zz).wait_recv()
                near = [ins[p].at[zz * 2 + y], from_row[p].at[zz]]

                @pl.when(has_left)
                def _():
                    right(p, zz).wait_recv()
                    add_rows(leaving[p].at[zz], near + [from_left[p].at[zz]])

                @pl.when(jnp.logical_not(has_left))
                def _():
                    add_rows(leaving[p].at[zz], near)

                right(p, zz).start()

            @pl.when(zz < z)
            def _():
                across(p, zz).wait_recv()
                near = [ins[p].at[zz * 2 + y], from_row[p].at[zz]]

                @pl.when(has_right)
                def _():
                    left(p, zz).wait_recv()
                    add_rows(leaving[p].at[zz], near + [from_right[p].at[zz]])

                @pl.when(jnp.logical_not(has_right))
                def _():
                    add_rows(leaving[p].at[zz], near)

                left(p, zz).start()

    for p in range(2):
        across(p, z).wait_recv()
        add_rows(outs[p], [ins[p].at[me], from_row[p].at[z]])

        @pl.when(has_left)
        def _():
            right(p, z).wait_recv()
            add_rows(outs[p], [outs[p], from_left[p].at[z]])

        @pl.when(has_right)
        def _():
            left(p, z).wait_recv()
            add_rows(outs[p], [outs[p], from_right[p].at[z]])

        for zz in range(m):
            across(p, zz).wait_send()

            @pl.when(z < zz)
            def _():
                right(p, zz).wait_send()

            @pl.when(z > zz)
            def _():
                left(p, zz).wait_send()


def backward(acts, grad_out, grad_query, attn_out, key_grad, value_grad, low, width, all_heads, share_rows, count, collective_id):
    layers, tokens, _ = acts.shape
    half, m = low.shape[2] // 8, count // 2
    dma = pltpu.SemaphoreType.DMA
    anywhere, vmem = pl.BlockSpec(memory_space=pl.ANY), pl.BlockSpec(memory_space=pltpu.VMEM)
    wide = (layers * width, 2 * half)
    head = (layers * all_heads * share_rows, half)
    slots = [pltpu.VMEM((m,) + shape, jnp.bfloat16) for shape in (wide, head)]
    return pl.pallas_call(
        functools.partial(backward_kernel, count, share_rows),
        out_shape=[jax.ShapeDtypeStruct(shape, jnp.float32) for shape in (wide, head)],
        in_specs=[anywhere] * 4 + [vmem] * 3,
        out_specs=[vmem] * 2,
        scratch_shapes=[pltpu.VMEM((count,) + shape, jnp.bfloat16) for shape in (wide, head)]
        + [
            pltpu.VMEM((count, layers, tokens, width), acts.dtype),
            pltpu.VMEM((count, layers, tokens, width), acts.dtype),
            pltpu.VMEM(grad_query.shape, grad_query.dtype),
            pltpu.VMEM(attn_out.shape, attn_out.dtype),
        ]
        + slots * 4
        + [dma((count,)), dma((count,)), dma((layers,)), dma((layers,))]
        + [dma((2, m))] * 5,
        compiler_params=pltpu.CompilerParams(
            collective_id=collective_id, has_side_effects=True, vmem_limit_bytes=48 * 2**20
        ),
        name="gradients_to_owners",
    )(acts, grad_out, grad_query, attn_out, key_grad, value_grad, low)


def merge_kernel(heads, away_ref, near_ref, mix, here, there, up_here, up_there, down, out):
    away = away_ref[pl.program_id(1)]
    count, share_rows = up_here.shape[0], up_here.shape[1] // heads

    def run(base, up):
        for h in range(heads):
            if share_rows % 16 == 0:
                rows = [up[slot, h * share_rows : (h + 1) * share_rows, :] for slot in range(count)]
            else:
                rows = [
                    up[slot].astype(jnp.float32)[h * share_rows : (h + 1) * share_rows]
                    for slot in range(count)
                ]
            ups = jnp.concatenate(rows, axis=0).astype(jnp.bfloat16)
            mixed_up = (adapter_scale * product(mix[...], ups)).astype(jnp.bfloat16)
            left = jnp.concatenate([mix[...], mixed_up], axis=1)
            right = jnp.concatenate([base[0, h], down[0]], axis=0)
            out[0, h] = product(left, right).astype(jnp.bfloat16)

    @pl.when(away == 0)
    def _():
        run(here, up_here)

    @pl.when(away != 0)
    def _():
        run(there, up_there)


def merge(base_here, base_there, up_here, up_there, down, mix, away, near, low_head, share_rows):
    layers, head_count, size, width = base_here.shape
    count, _, ranks = up_here.shape
    slots = away.shape[0]
    per_slot = head_count // slots
    heads = min(8, per_slot)
    steps = per_slot // heads

    def here_map(l, g, c, away, near):
        return jnp.where(away[g] == 0, l, 0), jnp.where(away[g] == 0, near[g] * steps + c, 0), 0, 0

    def there_map(l, g, c, away, near):
        return jnp.where(away[g] == 0, 0, l), jnp.where(away[g] == 0, 0, near[g] * steps + c), 0, 0

    def slot_map(l, g, c, away, near):
        return l, g * steps + c, 0, 0

    def up_map(l, g, c, away, near):
        return 0, low_head // heads + near[g] * steps + c, 0

    block = (1, heads, size, width)
    up_block = (count, heads * share_rows, ranks)
    return pl.pallas_call(
        functools.partial(merge_kernel, heads),
        out_shape=jax.ShapeDtypeStruct(base_here.shape, base_here.dtype),
        grid_spec=pltpu.PrefetchScalarGridSpec(
            num_scalar_prefetch=2,
            grid=(layers, slots, steps),
            in_specs=[
                pl.BlockSpec((size, size), lambda l, g, c, away, near: (0, 0)),
                pl.BlockSpec(block, here_map),
                pl.BlockSpec(block, there_map),
                pl.BlockSpec(up_block, up_map),
                pl.BlockSpec(up_block, up_map),
                pl.BlockSpec((1,) + down.shape[1:], lambda l, g, c, away, near: (l, 0, 0)),
            ],
            out_specs=pl.BlockSpec(block, slot_map),
        ),
        compiler_params=pltpu.CompilerParams(vmem_limit_bytes=40 * 2**20),
        name="merged_rows",
    )(away, near, mix, base_here, base_there, up_here, up_there, down)


def swap_core(value):
    return lax.ppermute(value, "tensor", [(0, 1), (1, 0)])


def body(
    acts,
    grad_query,
    keyvalue_gradient,
    attn_out,
    grad_out,
    seq_lengths,
    group_ids,
    rewards,
    wide_params,
    wide_moments,
    head_params,
    head_moments,
    key_value_adapters,
    kv_moments,
    base_query,
    frozen_key_rows,
    rotary_rows,
    rollout_group_order,
):
    count = lax.axis_size("dp")
    tensor_pos = lax.axis_index("tensor")
    layers, tokens, model_width = acts.shape
    wide_rows = wide_params.shape[1]
    rank = wide_params.shape[2] // 4
    heads, share_rows = head_params.shape[1:3]
    kv_heads = key_value_adapters.shape[1]
    all_heads = heads + kv_heads
    base_there = swap_core(base_query)
    frozen_there = swap_core(frozen_key_rows)

    wide_bf = wide_params.astype(jnp.bfloat16).reshape(-1, 4 * rank)
    head_bf = jnp.concatenate([head_params, key_value_adapters], axis=1).astype(jnp.bfloat16)
    weight_col = token_weights(seq_lengths, group_ids, rewards, tokens)[:, None]
    key_grad, value_grad = keyvalue_gradient[:, :, 0], keyvalue_gradient[:, :, 1]
    rows = (acts, grad_out, grad_query, attn_out, key_grad, value_grad)
    low = forward(
        wide_bf, head_bf.reshape(-1, 2 * rank), *rows, weight_col, count, share_rows, 0
    )
    wide_sum, head_sum = backward(*rows, low, wide_rows, all_heads, share_rows, count, 1)
    wide_grad = wide_sum.reshape(wide_params.shape)
    head_sum = head_sum.reshape(layers, all_heads, share_rows, 2 * rank)
    new_wide, new_wide_moments = adamw(wide_params, wide_moments, wide_grad)
    new_head, new_head_moments = adamw(head_params, head_moments, head_sum[:, :heads])
    new_kv, new_kv_moments = adamw(key_value_adapters, kv_moments, head_sum[:, heads:])

    up_own = jnp.concatenate([new_head[..., :rank], new_kv[..., :rank]], axis=1).astype(jnp.bfloat16)
    down_own = new_wide[..., : 2 * rank].astype(jnp.bfloat16)
    up_here, up_there, down_there = gather_dp(
        [jnp.concatenate(list(up_own), axis=-1).reshape(-1, layers * rank)], [down_own.reshape(-1, 2 * rank)], count, True, 2
    )
    down_there = down_there.reshape(down_own.shape)
    first = tensor_pos == 0
    rank_down = jnp.concatenate(
        [jnp.where(first, down_own, down_there), jnp.where(first, down_there, down_own)], axis=1
    ).transpose(0, 2, 1)

    slot_groups = kv_heads
    group_slots = tensor_pos * slot_groups + jnp.arange(slot_groups, dtype=jnp.int32)
    source_groups = jnp.take(rollout_group_order, group_slots)
    away = (source_groups // slot_groups != tensor_pos).astype(jnp.int32)
    near = (source_groups % slot_groups).astype(jnp.int32)

    same_layer = jnp.eye(layers, dtype=jnp.bfloat16)[:, :, None, None]

    def own_layer(part):
        return (same_layer * part[:, None]).reshape(layers, layers * rank, -1)

    down_query, down_key = own_layer(rank_down[:, :rank]), own_layer(rank_down[:, rank:])
    mix = (rotary_rows[:, None] == jnp.arange(rotary_rows.shape[0], dtype=jnp.int32)[None, :]).astype(
        jnp.bfloat16
    )
    merged_query = merge(
        base_query, base_there, up_here, up_there, down_query, mix, away, near, 0, share_rows
    )
    merged_key = merge(
        frozen_key_rows,
        frozen_there,
        up_here,
        up_there,
        down_key,
        mix,
        away,
        near,
        heads,
        share_rows,
    )
    return (
        new_wide,
        new_wide_moments,
        new_head,
        new_head_moments,
        new_kv,
        new_kv_moments,
        merged_query,
        merged_key,
    )


def solution(mesh):
    placed = (
        P("groups", "dp", None),
        P("groups", "dp", "tensor"),
        P("groups", "dp", None, "tensor"),
        P("groups", "dp", "tensor"),
        P("groups", "dp", None),
        P("dp", "groups"),
        P("dp", "groups"),
        P("dp", "groups"),
        P("groups", ("dp", "tensor"), None),
        P(None, "groups", ("dp", "tensor"), None),
        P("groups", "tensor", "dp", None),
        P(None, "groups", "tensor", "dp", None),
        P("groups", "tensor", "dp", None),
        P(None, "groups", "tensor", "dp", None),
        P(None, "tensor", None, "dp"),
        P(None, "tensor", None, "dp"),
        P(),
        P(),
    )
    return jax.shard_map(
        body,
        mesh=mesh,
        in_specs=placed,
        out_specs=(
            P("groups", ("dp", "tensor"), None),
            P(None, "groups", ("dp", "tensor"), None),
            P("groups", "tensor", "dp", None),
            P(None, "groups", "tensor", "dp", None),
            P("groups", "tensor", "dp", None),
            P(None, "groups", "tensor", "dp", None),
            P("groups", "tensor", None, "dp"),
            P("groups", "tensor", None, "dp"),
        ),
        check_vma=False,
    )
```
